1024 devices in a mesh: grp: 16 (over y, core), aa: 64 (over x, z).
Axes of the slice: x: 8, y: 8, z: 8, core: 2. Of those that a mesh axis runs over, the one named last changes fastest.
Arguments:
- spectrum: float32 [1600, 2048, 128], P(None, ('grp', 'aa')), may hold values from 0.05 to 2
- friction: float32 [2048, 128], P(('grp', 'aa')), may hold values from 0.2 to 1
- wind_dir: float32 [2048, 128], P(('grp', 'aa')), may hold values from -3.140625 to 3.140625
- wet: int32 [2048, 128], P('grp'), may hold values 0 or 1
- owner: int32 [262144, 1], P(('grp', 'aa')), may hold values from 0 to 15; in each aligned block of 256 rows (0 to 255, 256 to 511, ...) at most 32 rows name the same one
- cell: int32 [2048, 128], P(('grp', 'aa')), may hold values from 0 to 255
Outputs:
- new_spectrum: float32 [1600, 2048, 128], P(None, ('grp', 'aa'))
- forcing: float32 [3, 262144], P(None, ('grp', 'aa'))
The draws below stay inside these ranges and needn't reach their ends.
Inputs may be any that keep to these rules, and one draw needn't show every extreme that they name: Among the 256 points of one device no owner is named more than 32 times; some owner is named exactly 32 times.
All inputs are finite; a program needn't handle non-finite values. No bound on the sum of `wet` on one device may be relied on, other than what follows from the above.
Results may differ from the reference program's by a relative error of at most 0.0001.
Values sent between devices are 32-bit elements; how exact they have to be, the bound alone decides.
A program may use at most 32 MiB of HBM per device.

```python
import math
import jax
import jax.numpy as jnp
import numpy as np
from jax import lax

FREQS = 50
DIRS = 32
RDEV = 2
GX = 128
ITERS = 2
OC_TILE = 256
COMPS = 1600
NY = 2048
NPTS = 262144
P_DEV = 256
CAP = 32
N_GRP = 16
N_AA = 64


def touch_ends(array, stream_key, least, high):
    longest = array.shape.index(max(array.shape))
    spots = []
    for shift in (0, 1):
        where = [jax.random.randint(jax.random.fold_in(stream_key, axis), (), 0, length) for axis, length in enumerate(array.shape)]
        where[longest] = (where[longest] + shift) % array.shape[longest]
        spots.append(tuple(where))
    return array.at[spots[0]].set(least).at[spots[1]].set(high)


def block_levels(key, extent, pieces, low, largest):
    loudness = 1.0
    for dim, parts in pieces:
        steps = jax.random.uniform(jax.random.fold_in(jax.random.fold_in(key, 6), dim), (parts,), jnp.float32, low / len(pieces), largest / len(pieces))
        loudness = loudness * jnp.repeat(jnp.exp(steps), extent[dim] // parts).reshape((-1,) + (1,) * (len(extent) - 1 - dim))
    return loudness


def routed_block(own_key, own, number, rows, amount, top, most, lean):
    sequence = jax.random.permutation(own_key, amount)
    heavy_load, common = load_shares(amount, rows * top, most, lean, True), load_shares(amount, rows * top, most, lean, False)
    places = jnp.arange(amount)

    def named(sizes, rotation):
        used = int((sizes > 0).sum())
        fixed = max(1, used // 4)
        moved = fixed + (places - fixed + rotation * (used - fixed)) % max(1, amount - fixed)
        return jnp.zeros((amount,), jnp.int32).at[sequence[jnp.where(places < fixed, places, moved)]].set(jnp.asarray(sizes, jnp.int32))

    sizes = jnp.where(number % 4 == 0, named(heavy_load, number // 4), named(common, number - number // 4 - 1))
    mixed = jax.random.permutation(jax.random.fold_in(own, 3), amount)
    giver, sink = mixed[0:amount // 2 * 2:2], mixed[1:amount // 2 * 2:2]
    margin = jnp.minimum(sizes[giver] - 1, most - sizes[sink]) // 2
    margin = jnp.where((giver == sequence[0]) | (sink == sequence[0]) | (sizes[sink] == 0), 0, jnp.maximum(margin, 0))
    moved = jax.random.randint(jax.random.fold_in(own, 4), (amount // 2,), 0, 1 << 20) % (margin + 1)
    sizes = sizes.at[giver].add(-moved).at[sink].add(moved)
    labels = jnp.searchsorted(jnp.cumsum(sizes), jnp.arange(rows * top), side="right").astype(jnp.int32)
    listing = labels.reshape(top, rows).T
    listing = listing[jax.random.permutation(jax.random.fold_in(own, 1), rows)]
    rotation = jax.random.randint(jax.random.fold_in(own, 2), (rows, 1), 0, top)
    return jnp.take_along_axis(listing, (jnp.arange(top)[None, :] + rotation) % top, axis=1)


def load_shares(number_of, total, limit, lean, full):
    weights = [(1 << 20) // math.isqrt(standing ** lean) + 1 for standing in range(1, number_of + 1)]
    largest = limit if full else min(limit, max(-(-total // number_of), total * weights[0] // sum(weights)))
    least = 1 if total - largest >= number_of - 1 else 0
    given, rest = [largest] + [least] * (number_of - 1), total - largest - least * (number_of - 1)
    while rest > 0:
        movable = [i for i in range(1, number_of) if given[i] < largest] or [i for i in range(1, number_of) if given[i] < limit]
        mass, left = sum([weights[i] for i in movable]), rest
        for i in movable:
            more = min(limit - given[i], max(1, left * weights[i] // mass), rest)
            given[i] = given[i] + more
            rest = rest - more
    return np.array(given)


def setup_inputs(seed: int = 0) -> dict:
    splits = jax.random.split(jax.random.key(seed), 7)
    spectrum = jnp.clip(jnp.exp(math.log(2.0) - 3.6888794 * jax.random.uniform(splits[0], (COMPS, NY, GX), jnp.float32) ** block_levels(splits[0], (COMPS, NY, GX), ((1, 1024),), -0.2, 0.2)), 0.05, 2.0)
    friction = jnp.clip(jnp.exp(math.log(1.0) - 1.609438 * jax.random.uniform(splits[1], (NY, GX), jnp.float32) ** block_levels(splits[1], (NY, GX), ((0, 1024),), -0.2, 0.2)), 0.2, 1.0)
    wind_dir = jnp.clip(jax.random.uniform(splits[2], (NY, GX), jnp.float32, -3.140625, 3.140625), -3.140625, 3.140625)
    wet = touch_ends((jax.random.randint(splits[3], (NY, GX), 0, 5) < 4).astype(jnp.int32), jax.random.fold_in(splits[3], 1), 0, 1)
    owner_keys = jax.random.split(jax.random.fold_in(splits[4], 1), NPTS // P_DEV)
    owner_turns = jax.random.permutation(jax.random.fold_in(splits[4], 3), NPTS // P_DEV)
    owner = jax.vmap(lambda own, number: routed_block(jax.random.fold_in(splits[4], 2), own, number, P_DEV, N_GRP, 1, CAP, 2))(owner_keys, owner_turns).reshape((NPTS, 1))
    cell = touch_ends(jax.random.randint(splits[5], (NY, GX), 0, OC_TILE), jax.random.fold_in(splits[5], 1), 0, OC_TILE - 1).astype(jnp.int32)
    return {"spectrum": spectrum, "friction": friction, "wind_dir": wind_dir, "wet": wet, "owner": owner, "cell": cell}


COURANT = 0.7


def spectral_tables(count):
    index = jnp.arange(count, dtype=jnp.int32)
    freq_index = (index // DIRS).astype(jnp.float32)
    dir_index = (index % DIRS).astype(jnp.float32)
    relative = freq_index / jnp.float32(max(FREQS - 1, 1))
    angle = jnp.float32(2.0 * math.pi) * dir_index / jnp.float32(DIRS)
    speed = jnp.power(jnp.float32(0.5), relative)
    return relative, angle, speed


def source_terms(spectrum, total, friction, wind_dir, wetness, relative, angle):
    growth = 0.4 * friction[None] * (0.5 + relative)[:, None, None] * jnp.maximum(jnp.cos(angle[:, None, None] - wind_dir[None]), 0.0)
    damping = 0.6 * (0.25 + relative)[:, None, None] * (total / (1.0 + total))[None]
    return wetness[None] * spectrum * jnp.exp(growth - damping)


def advect(padded, courant_x, courant_y):
    center = padded[:, 1:-1]
    south = padded[:, :-2]
    north = padded[:, 2:]
    side = jnp.pad(center, ((0, 0), (0, 0), (1, 1)))
    west = side[:, :, :-2]
    east = side[:, :, 2:]
    speed_x = courant_x[:, None, None]
    speed_y = courant_y[:, None, None]
    return (center - jnp.maximum(speed_x, 0.0) * (center - west) - jnp.minimum(speed_x, 0.0) * (east - center)
            - jnp.maximum(speed_y, 0.0) * (center - south) - jnp.minimum(speed_y, 0.0) * (north - center))


def stress_weights(angle, count):
    cosine = jnp.cos(angle)
    sine = jnp.sin(angle)
    return jnp.stack([0.5 * cosine * cosine, 0.5 * cosine * sine, 0.5 * sine * sine]) / jnp.float32(count)


def reference(spectrum, friction, wind_dir, wet, owner, cell):
    count = DIRS * FREQS
    wetness = wet.astype(jnp.float32)
    relative, angle, speed = spectral_tables(count)
    total = jnp.mean(spectrum, axis=0)
    width = count // N_AA

    def run_block(carry, items):
        piece, rel_part, ang_part, spd_part = items
        energy = source_terms(piece, total, friction, wind_dir, wetness, rel_part, ang_part)
        for substep in range(ITERS):
            padded = jnp.pad(energy, ((0, 0), (1, 1), (0, 0)))
            energy = wetness[None] * advect(padded, COURANT * spd_part * jnp.cos(ang_part), COURANT * spd_part * jnp.sin(ang_part))
        weights = stress_weights(ang_part, count)
        carry = carry + jnp.dot(weights, energy.reshape(energy.shape[0], -1), precision=lax.Precision.HIGHEST)
        return carry, energy

    stress, blocks = lax.scan(run_block, jnp.zeros((3, NY * GX), jnp.float32),
                              (spectrum.reshape(N_AA, width, NY, GX), relative.reshape(N_AA, width),
                               angle.reshape(N_AA, width), speed.reshape(N_AA, width)))
    new_spectrum = blocks.reshape(count, NY, GX)
    rows = jnp.arange(NY * GX, dtype=jnp.int32) // GX
    column = (rows // RDEV) % N_AA
    flat = (owner[:, 0] * N_AA + column) * OC_TILE + cell.reshape(-1)
    forcing = jax.ops.segment_sum(stress.T, flat, num_segments=OC_TILE * N_GRP * N_AA).T
    return new_spectrum, forcing
```

```python
import functools
import math

import jax
import jax.numpy as jnp
from jax import lax
from jax.experimental import pallas as pl
from jax.experimental.pallas import tpu as pltpu
from jax.sharding import PartitionSpec as P

MESH = pl.DeviceIdType.MESH
DIRS = 32
COURANT = 0.7
LOG2E = math.log2(math.e)
CHUNK = 2
WINDOW = 25
LOADS = 5
F32 = jnp.float32

EDGE = (1, 1, 0, 0)
WEST = (True, False, False, True)


def row(ref, index):
    return ref[pl.ds(index, 1), :]


def roll_up(cells, west):
    return pltpu.roll(cells, 1 if west else 127, 1)


def kernel(
    freqs,
    spectrum_hbm,
    friction_hbm,
    wind_hbm,
    wet_hbm,
    owner_hbm,
    cell_hbm,
    out_hbm,
    forcing_ref,
    spectrum,
    friction,
    wind,
    wet,
    owner,
    cell,
    stepped,
    send_up,
    send_down,
    got_up,
    got_down,
    inner,
    coefs,
    scales,
    moments,
    edge_send,
    edge_got,
    parts,
    parts_got,
    load_sem,
    small_sem,
    up_send_sem,
    up_recv_sem,
    down_send_sem,
    down_recv_sem,
    edge_send_sem,
    edge_recv_sem,
    part_send_sem,
    part_recv_sem,
    out_sem,
):
    groups, column = lax.axis_size("grp"), lax.axis_size("aa")
    my_grp, my_aa = lax.axis_index("grp"), lax.axis_index("aa")
    devices = groups * column
    me = my_grp * column + my_aa
    after = lax.rem(me + 1, devices)
    before = lax.rem(me + devices - 1, devices)
    next_id = (after // column, lax.rem(after, column))
    prev_id = (before // column, lax.rem(before, column))
    chunks = freqs // CHUNK
    rows_all = spectrum.shape[0]
    piece = rows_all // LOADS

    loads = [
        pltpu.make_async_copy(
            spectrum_hbm.at[pl.ds(i * piece, piece)], spectrum.at[pl.ds(i * piece, piece)], load_sem.at[i]
        )
        for i in range(LOADS)
    ]
    wet_start = pl.multiple_of((2 * my_aa) // 8 * 8, 8)
    smalls = [
        pltpu.make_async_copy(friction_hbm, friction, small_sem.at[0]),
        pltpu.make_async_copy(wind_hbm, wind, small_sem.at[1]),
        pltpu.make_async_copy(wet_hbm.at[pl.ds(wet_start, 8)], wet, small_sem.at[2]),
        pltpu.make_async_copy(owner_hbm, owner, small_sem.at[3]),
        pltpu.make_async_copy(cell_hbm, cell, small_sem.at[4]),
    ]
    for copy in smalls[:3] + loads + smalls[3:]:
        copy.start()
    barrier = pltpu.get_barrier_semaphore()
    for neighbour in (next_id, prev_id):
        pl.semaphore_signal(barrier, inc=1, device_id=neighbour, device_id_type=MESH)
    for turn in range(1, groups):
        peer = lax.rem(my_grp + turn, groups)
        pl.semaphore_signal(barrier, inc=1, device_id=(peer, my_aa), device_id_type=MESH)

    lane = lax.broadcasted_iota(jnp.int32, (8, 128), 1)
    turn8 = lax.broadcasted_iota(jnp.int32, (8, 128), 0)
    cos0 = jnp.full((8, 128), 1.0, F32)
    sin0 = jnp.full((8, 128), 0.0, F32)
    for j in range(1, 8):
        cos0 = jnp.where(turn8 == j, F32(math.cos(2.0 * math.pi * j / DIRS)), cos0)
        sin0 = jnp.where(turn8 == j, F32(math.sin(2.0 * math.pi * j / DIRS)), sin0)
    cosine = (cos0, -sin0, -cos0, sin0)
    sine = (sin0, cos0, -sin0, -cos0)
    abs_x = [COURANT * c for c in (cos0, sin0, cos0, sin0)]
    abs_y = [COURANT * c for c in (sin0, cos0, sin0, cos0)]
    speed_sum = COURANT * (cos0 + sin0)
    side = [jnp.where(lane != 0, 1.0, 0.0) if west else jnp.where(lane != 127, 1.0, 0.0) for west in WEST]

    number = lax.broadcasted_iota(jnp.int32, scales.shape[1:], 0).astype(F32) * F32(1.0 / max(freqs - 1, 1))
    scales[0] = number
    scales[1] = jnp.exp2(-number)
    moments[...] = jnp.zeros_like(moments)
    edge_send[...] = jnp.zeros_like(edge_send)

    for copy in smalls[:3]:
        copy.wait()
    has = [jnp.where(me > 0, 1.0, 0.0).astype(F32), jnp.where(me < devices - 1, 1.0, 0.0).astype(F32)]
    wet_row = lax.rem(2 * my_aa, 8)
    wetness = [jnp.broadcast_to(row(wet, wet_row + y).astype(F32), (8, 128)) for y in range(2)]
    wind_cos, wind_sin = jnp.cos(wind[...]), jnp.sin(wind[...])
    grow = [
        [
            0.4
            * friction[y : y + 1, :]
            * jnp.maximum(cosine[g] * wind_cos[y : y + 1, :] + sine[g] * wind_sin[y : y + 1, :], 0.0)
            for y in range(2)
        ]
        for g in range(4)
    ]

    acc = jnp.zeros((8, 128), F32)
    for i in range(LOADS):
        loads[i].wait()
        tiles = piece // 64

        def add(t, acc, i=i):
            at = pl.multiple_of(i * piece + t * 64, 64)
            return acc + jnp.sum(spectrum[pl.ds(at, 64), :].reshape(8, 8, 128), axis=0)

        acc = lax.fori_loop(0, tiles, add, acc, unroll=2)
    parity = lax.rem(turn8, 2)
    total = [
        jnp.sum(jnp.where(parity == y, acc, 0.0), axis=0, keepdims=True) / F32(rows_all // 2) for y in range(2)
    ]
    damp = [t / (1.0 + t) for t in total]

    for g in range(4):
        for y in range(2):
            coefs[0, g * 2 + y] = LOG2E * (0.5 * grow[g][y] - 0.15 * damp[y])
            coefs[1, g * 2 + y] = LOG2E * (grow[g][y] - 0.6 * damp[y])
            coefs[2, g * 2 + y] = wetness[y] * side[g] * abs_x[g]
            pull = wetness[y] * abs_y[g]
            if y != EDGE[g]:
                pull = pull * (has[0] if g < 2 else has[1])
            coefs[3, g * 2 + y] = pull
    coefs[4, 0] = wetness[0]
    coefs[4, 1] = wetness[1]
    coefs[4, 2] = speed_sum

    def scale(index, k):
        return jnp.broadcast_to(scales[index, pl.ds(k, 1), :], (8, 128))

    def slope(g, y, cells, other):
        pulled = coefs[2, g * 2 + y] * roll_up(cells, WEST[g])
        if other is not None:
            pulled = pulled + coefs[3, g * 2 + y] * other
        return coefs[4, 2] * cells - pulled

    pl.semaphore_wait(barrier, groups + 1)

    def copies(c):
        return (
            pltpu.make_async_remote_copy(
                src_ref=send_up.at[c],
                dst_ref=got_up.at[c],
                send_sem=up_send_sem.at[c],
                recv_sem=up_recv_sem.at[c],
                device_id=next_id,
                device_id_type=MESH,
            ),
            pltpu.make_async_remote_copy(
                src_ref=send_down.at[c],
                dst_ref=got_down.at[c],
                send_sem=down_send_sem.at[c],
                recv_sem=down_recv_sem.at[c],
                device_id=prev_id,
                device_id_type=MESH,
            ),
        )

    def start(c):
        for copy in copies(c):
            copy.start()

    def make(c, carry):
        for g in range(4):
            e = EDGE[g]
            o = 1 - e
            sums = [[moments[g * 6 + y * 3 + m] for m in range(3)] for y in range(2)]
            for kk in range(CHUNK):
                k = c * CHUNK + kk
                base = k * 64 + g * 16
                q, s = scale(0, k), scale(1, k)
                energy = []
                for y in range(2):
                    cells = spectrum[pl.ds(base + y, 8, stride=2), :]
                    power = jnp.exp2(coefs[0, g * 2 + y] + q * coefs[1, g * 2 + y])
                    energy.append(coefs[4, y] * cells * power)
                    first = s * energy[y]
                    sums[y][0] = sums[y][0] + energy[y]
                    sums[y][1] = sums[y][1] + first
                    sums[y][2] = sums[y][2] + s * first
                step = energy[e] - s * slope(g, e, energy[e], energy[o])
                send = send_up if g < 2 else send_down
                at = (kk * 2 + g % 2) * 16
                send[c, pl.ds(at, 8), :] = energy[e]
                send[c, pl.ds(at + 8, 8), :] = step
                inner[c, pl.ds((kk * 4 + g) * 8, 8), :] = energy[o]
            for y in range(2):
                for m in range(3):
                    moments[g * 6 + y * 3 + m] = sums[y][m]

        @pl.when(c < WINDOW)
        def _():
            start(c)

        return carry

    lax.fori_loop(0, chunks, make, 0)

    def weigh(g):
        per = F32(1.0 / (rows_all // 2))
        return (
            0.5 * per * cosine[g] * cosine[g],
            0.5 * per * cosine[g] * sine[g],
            0.5 * per * sine[g] * sine[g],
        )

    def reduce8(cells):
        return jnp.sum(cells, axis=0, keepdims=True)

    own = [[jnp.zeros((8, 128), F32) for _ in range(2)] for _ in range(3)]
    for d in range(2):
        direct = [jnp.zeros((8, 128), F32) for _ in range(3)]
        double = [jnp.zeros((8, 128), F32) for _ in range(3)]
        for gi in range(2):
            g = 2 * d + gi
            e = EDGE[g]
            o = 1 - e
            m_e = [moments[g * 6 + e * 3 + m] for m in range(3)]
            m_o = [moments[g * 6 + o * 3 + m] for m in range(3)]
            slope_o2 = slope(g, o, m_o[2], None)
            slope_e2 = slope(g, e, m_e[2], m_o[2])
            sum_o = m_o[0] - 2.0 * slope(g, o, m_o[1], None) + slope(g, o, slope_o2, None)
            sum_e = m_e[0] - 2.0 * slope(g, e, m_e[1], m_o[1]) + slope(g, e, slope_e2, slope_o2)
            weights = weigh(g)
            reach = abs_y[g] * (2.0 * m_e[1] - speed_sum * m_e[2] - slope_e2)
            sideways = abs_x[g] * abs_y[g] * m_e[2]
            twice = abs_y[g] * abs_y[g] * m_e[2]
            for i in range(3):
                own[i][e] = own[i][e] + weights[i] * sum_e
                own[i][o] = own[i][o] + weights[i] * sum_o
                direct[i] = direct[i] + weights[i] * reach
                double[i] = double[i] + weights[i] * twice
                edge_send[d, 8 + gi * 3 + i : 9 + gi * 3 + i, :] = reduce8(weights[i] * sideways)
        for i in range(3):
            edge_send[d, i : i + 1, :] = reduce8(direct[i])
            edge_send[d, 3 + i : 4 + i, :] = reduce8(double[i])
    edges = [
        pltpu.make_async_remote_copy(
            src_ref=edge_send.at[d],
            dst_ref=edge_got.at[d],
            send_sem=edge_send_sem.at[d],
            recv_sem=edge_recv_sem.at[d],
            device_id=next_id if d == 0 else prev_id,
            device_id_type=MESH,
        )
        for d in range(2)
    ]
    for copy in edges:
        copy.start()
    stress = [[reduce8(own[i][y]) for y in range(2)] for i in range(3)]

    def finish(c, carry):
        @pl.when(c + WINDOW < chunks)
        def _():
            start(c + WINDOW)

        for copy in copies(c):
            copy.wait_recv()
        for kk in range(CHUNK):
            for g in range(4):
                e = EDGE[g]
                o = 1 - e
                k = c * CHUNK + kk
                s = scale(1, k)
                send = send_up if g < 2 else send_down
                got = got_up if g < 2 else got_down
                at = (kk * 2 + g % 2) * 16
                start_o = inner[c, pl.ds((kk * 4 + g) * 8, 8), :]
                one_e = send[c, pl.ds(at + 8, 8), :]
                one_o = start_o - s * slope(g, o, start_o, got[c, pl.ds(at, 8), :])
                two_o = one_o - s * slope(g, o, one_o, got[c, pl.ds(at + 8, 8), :])
                two_e = one_e - s * slope(g, e, one_e, one_o)
                base = k * 64 + g * 16
                stepped[pl.ds(base + o, 8, stride=2), :] = two_o
                stepped[pl.ds(base + e, 8, stride=2), :] = two_e
        put(c).start()
        return carry

    def put(c):
        at = pl.multiple_of(c * (CHUNK * 64), 64)
        return pltpu.make_async_copy(
            stepped.at[pl.ds(at, CHUNK * 64)], out_hbm.at[pl.ds(at, CHUNK * 64)], out_sem.at[c]
        )

    first_stop, second_stop = chunks // 4, (3 * chunks) // 4
    lax.fori_loop(0, first_stop, finish, 0)

    for copy in edges:
        copy.wait_recv()
    for copy in smalls[3:]:
        copy.wait()
    for d in range(2):
        o, e = d, 1 - d
        here = has[d] * coefs[4, o][:1]
        both = here * coefs[4, e][:1]
        sideways = edge_got[d, 8:16, :] * coefs[4, o]
        for i in range(3):
            moved = edge_got[d, i : i + 1, :]
            for gi in range(2):
                g = 2 * d + gi
                moved = moved + (side[g] * roll_up(sideways, WEST[g]))[gi * 3 + i : gi * 3 + i + 1]
            stress[i][o] = stress[i][o] + here * moved
            stress[i][e] = stress[i][e] + both * edge_got[d, 3 + i : 4 + i, :]

    target = lax.broadcasted_iota(jnp.int32, (groups * 8, 128), 0)
    place = lax.broadcasted_iota(jnp.int32, (128, 128), 0)
    summed = jnp.zeros((groups * 8, 128), F32)
    for y in range(2):
        cells = cell[y : y + 1, :]
        high = jnp.where(cells >= 128, 1, 0)
        goal = owner[y : y + 1, :] * 8 + high * 3
        spread = jnp.zeros((groups * 8, 128), F32)
        for i in range(3):
            spread = jnp.where(target == goal + i, stress[i][y], spread)
        table = jnp.where(place == cells - high * 128, 1.0, 0.0).astype(F32)
        summed = summed + lax.dot_general(
            spread,
            table,
            (((1,), (1,)), ((), ())),
            precision=lax.Precision.HIGHEST,
            preferred_element_type=F32,
        )
    parts[...] = summed.reshape(groups, 8, 128)

    def part(turn):
        peer = lax.rem(my_grp + turn, groups)
        return pltpu.make_async_remote_copy(
            src_ref=parts.at[peer],
            dst_ref=parts_got.at[turn],
            send_sem=part_send_sem.at[turn],
            recv_sem=part_recv_sem.at[turn],
            device_id=(peer, my_aa),
            device_id_type=MESH,
        )

    for turn in range(1, groups):
        part(turn).start()

    lax.fori_loop(first_stop, second_stop, finish, 0)

    forcing = parts[my_grp]
    for turn in range(1, groups):
        part(turn).wait_recv()
        forcing = forcing + parts_got[turn]
    forcing_ref[:, 0:128] = forcing[0:3]
    forcing_ref[:, 128:256] = forcing[3:6]

    lax.fori_loop(second_stop, chunks, finish, 0)

    for turn in range(1, groups):
        part(turn).wait_send()
    for copy in edges:
        copy.wait_send()

    def drain(c, carry):
        for copy in copies(c):
            copy.wait_send()
        put(c).wait()
        return carry

    lax.fori_loop(0, chunks, drain, 0)


def on_device(groups, spectrum, friction, wind_dir, wet, owner, cell):
    comps, rows, width = spectrum.shape
    freqs = comps // DIRS
    chunks = freqs // CHUNK
    any_space = pl.BlockSpec(memory_space=pl.ANY)
    dma = pltpu.SemaphoreType.DMA
    new, forcing = pl.pallas_call(
        functools.partial(kernel, freqs),
        out_shape=(
            jax.ShapeDtypeStruct((comps * rows, width), F32),
            jax.ShapeDtypeStruct((3, 256), F32),
        ),
        in_specs=[any_space] * 6,
        out_specs=(any_space, pl.BlockSpec(memory_space=pltpu.VMEM)),
        scratch_shapes=[
            pltpu.VMEM((comps * rows, width), F32),
            pltpu.VMEM((rows, width), F32),
            pltpu.VMEM((rows, width), F32),
            pltpu.VMEM((8, width), jnp.int32),
            pltpu.VMEM((rows, width), jnp.int32),
            pltpu.VMEM((rows, width), jnp.int32),
            pltpu.VMEM((comps * rows, width), F32),
            pltpu.VMEM((chunks, CHUNK * 32, width), F32),
            pltpu.VMEM((chunks, CHUNK * 32, width), F32),
            pltpu.VMEM((chunks, CHUNK * 32, width), F32),
            pltpu.VMEM((chunks, CHUNK * 32, width), F32),
            pltpu.VMEM((chunks, CHUNK * 32, width), F32),
            pltpu.VMEM((5, 8, 8, width), F32),
            pltpu.VMEM((2, (freqs + 7) // 8 * 8, width), F32),
            pltpu.VMEM((24, 8, width), F32),
            pltpu.VMEM((2, 16, width), F32),
            pltpu.VMEM((2, 16, width), F32),
            pltpu.VMEM((groups, 8, width), F32),
            pltpu.VMEM((groups, 8, width), F32),
            dma((LOADS,)),
            dma((5,)),
            dma((chunks,)),
            dma((chunks,)),
            dma((chunks,)),
            dma((chunks,)),
            dma((2,)),
            dma((2,)),
            dma((groups,)),
            dma((groups,)),
            dma((chunks,)),
        ],
        compiler_params=pltpu.CompilerParams(
            collective_id=0, has_side_effects=True, vmem_limit_bytes=60 * 1024 * 1024
        ),
    )(
        spectrum.reshape(comps * rows, width),
        friction,
        wind_dir,
        wet,
        owner.reshape(rows, width),
        cell,
    )
    return new.reshape(comps, rows, width), forcing


def solution(mesh):
    placed = (
        P(None, ("grp", "aa"), None),
        P(("grp", "aa"), None),
        P(("grp", "aa"), None),
        P("grp", None),
        P(("grp", "aa"), None),
        P(("grp", "aa"), None),
    )
    return jax.shard_map(
        functools.partial(on_device, mesh.shape["grp"]),
        mesh=mesh,
        in_specs=placed,
        out_specs=(P(None, ("grp", "aa"), None), P(None, ("grp", "aa"))),
        check_vma=False,
    )
```

```python
import functools
import math

import jax
import jax.numpy as jnp
from jax import lax
from jax.experimental import pallas as pl
from jax.experimental.pallas import tpu as pltpu
from jax.sharding import PartitionSpec as P

MESH = pl.DeviceIdType.MESH
DIRS = 32
COURANT = 0.7
LOG2E = math.log2(math.e)
CHUNKS = (0, 15, 24, 33, 41, 47, 50)
FIRST, SECOND = 1, 3
PIECES = 4
LIMIT = 60 * 1024 * 1024
F32 = jnp.float32

EDGE = (1, 1, 0, 0)
WEST = (True, False, False, True)


def roll_up(cells, west):
    return pltpu.roll(cells, 1 if west else 127, 1)


def wide(cells):
    return jnp.broadcast_to(cells, (8, 128))


def reduce8(cells):
    return jnp.sum(cells, axis=0, keepdims=True)


def kernel(
    chunks,
    spectrum_hbm,
    friction_hbm,
    wind_hbm,
    wet_hbm,
    owner_hbm,
    cell_hbm,
    out_hbm,
    forcing_hbm,
    spectrum,
    friction,
    wind,
    wet,
    owner,
    cell,
    stepped,
    got,
    near,
    far,
    mine,
    others,
    coefs,
    halo,
    scales,
    moments,
    edge_send,
    edge_got,
    parts,
    parts_got,
    forcing,
    load_sem,
    small_sem,
    send_sem,
    recv_sem,
    tile_send_sem,
    tile_recv_sem,
    edge_send_sem,
    edge_recv_sem,
    part_send_sem,
    part_recv_sem,
    out_sem,
    forcing_sem,
    here_sem,
    all_sem,
):
    freqs = spectrum.shape[0]
    groups, column = lax.axis_size("grp"), lax.axis_size("aa")
    my_grp, my_aa = lax.axis_index("grp"), lax.axis_index("aa")
    devices = groups * column
    me = my_grp * column + my_aa
    after = lax.rem(me + 1, devices)
    before = lax.rem(me + devices - 1, devices)
    row_ids = ((after // column, lax.rem(after, column)), (before // column, lax.rem(before, column)))
    last = len(chunks) - 1

    barrier = pltpu.get_barrier_semaphore()
    for other in row_ids:
        pl.semaphore_signal(barrier, inc=1, device_id=other, device_id_type=MESH)

    @pl.when(my_grp == 0)
    def _():
        for peer in range(1, groups):
            pl.semaphore_signal(barrier, inc=1, device_id=(peer, my_aa), device_id_type=MESH)

    half = freqs // 2
    loads = [
        pltpu.make_async_copy(spectrum_hbm.at[pl.ds(i * half, half)], spectrum.at[pl.ds(i * half, half)], load_sem.at[i])
        for i in range(2)
    ]
    wet_start = pl.multiple_of((2 * my_aa) // 8 * 8, 8)
    smalls = [
        pltpu.make_async_copy(friction_hbm, friction, small_sem.at[0]),
        pltpu.make_async_copy(wind_hbm, wind, small_sem.at[1]),
        pltpu.make_async_copy(wet_hbm.at[pl.ds(wet_start, 8)], wet, small_sem.at[2]),
        pltpu.make_async_copy(owner_hbm, owner, small_sem.at[3]),
        pltpu.make_async_copy(cell_hbm, cell, small_sem.at[4]),
    ]
    for copy in smalls[:3] + loads + smalls[3:]:
        copy.start()
    pl.semaphore_wait(barrier, jnp.where(my_grp == 0, 2, 3))

    def bulk(d, c):
        where = pl.ds(chunks[c], chunks[c + 1] - chunks[c])
        return pltpu.make_async_remote_copy(
            src_ref=spectrum_hbm.at[where, pl.ds(32 * d, 32)],
            dst_ref=got.at[d, where],
            send_sem=send_sem.at[d],
            recv_sem=recv_sem.at[d, c],
            device_id=row_ids[d],
            device_id_type=MESH,
        )

    for d in range(2):
        bulk(d, 0).start()

    @pl.when(my_grp != 0)
    def _():
        pl.semaphore_signal(here_sem, inc=1, device_id=(0, my_aa), device_id_type=MESH)

    lane = lax.broadcasted_iota(jnp.int32, (8, 128), 1)
    place8 = lax.broadcasted_iota(jnp.int32, (8, 128), 0)
    cos0 = jnp.full((8, 128), 1.0, F32)
    sin0 = jnp.full((8, 128), 0.0, F32)
    for j in range(1, 8):
        cos0 = jnp.where(place8 == j, F32(math.cos(2.0 * math.pi * j / DIRS)), cos0)
        sin0 = jnp.where(place8 == j, F32(math.sin(2.0 * math.pi * j / DIRS)), sin0)
    cosine = (cos0, -sin0, -cos0, sin0)
    sine = (sin0, cos0, -sin0, -cos0)
    abs_x = [COURANT * c for c in (cos0, sin0, cos0, sin0)]
    abs_y = [COURANT * c for c in (sin0, cos0, sin0, cos0)]
    speed_sum = COURANT * (cos0 + sin0)
    side = [jnp.where(lane != 0, 1.0, 0.0) if west else jnp.where(lane != 127, 1.0, 0.0) for west in WEST]
    number = lax.broadcasted_iota(jnp.int32, scales.shape[1:], 0).astype(F32) * F32(1.0 / max(freqs - 1, 1))
    scales[0] = number
    scales[1] = jnp.exp2(-number)
    edge_send[...] = jnp.zeros_like(edge_send)
    has = [jnp.where(me > 0, 1.0, 0.0).astype(F32), jnp.where(me < devices - 1, 1.0, 0.0).astype(F32)]

    for copy in smalls[:3]:
        copy.wait()
    grow = 0.4 * friction[...]
    mine[0:2, :] = grow * jnp.cos(wind[...])
    mine[2:4, :] = grow * jnp.sin(wind[...])
    wet_row = lax.rem(2 * my_aa, 8)
    for y in range(2):
        mine[6 + y : 7 + y, :] = wet[pl.ds(wet_row + y, 1), :].astype(F32)

    def add(k, acc):
        return acc + jnp.sum(spectrum[k].reshape(8, 8, 128), axis=0)

    acc = jnp.zeros((8, 128), F32)
    for i in range(2):
        loads[i].wait()
        acc = lax.fori_loop(i * half, (i + 1) * half, add, acc)
    for y in range(2):
        total = reduce8(jnp.where(lax.rem(place8, 2) == y, acc, 0.0)) / F32(freqs * DIRS)
        mine[4 + y : 5 + y, :] = total / (1.0 + total)

    def tile(d):
        return pltpu.make_async_remote_copy(
            src_ref=mine,
            dst_ref=others.at[d],
            send_sem=tile_send_sem.at[d],
            recv_sem=tile_recv_sem.at[d],
            device_id=row_ids[d],
            device_id_type=MESH,
        )

    for d in range(2):
        tile(d).start()

    def exponent(values, g, y):
        growth = jnp.maximum(cosine[g] * values[0 + y : 1 + y] + sine[g] * values[2 + y : 3 + y], 0.0)
        damp = values[4 + y : 5 + y]
        return LOG2E * (0.5 * growth - 0.15 * damp), LOG2E * (growth - 0.6 * damp)

    values = mine[...]
    for g in range(4):
        for y in range(2):
            coefs[0, g * 2 + y], coefs[1, g * 2 + y] = exponent(values, g, y)
            coefs[2, g * 2 + y] = values[6 + y : 7 + y] * side[g] * abs_x[g]
            pull = values[6 + y : 7 + y] * abs_y[g]
            coefs[3, g * 2 + y] = pull if y == EDGE[g] else pull * has[g // 2]
    for y in range(2):
        coefs[4, y] = wide(values[6 + y : 7 + y])
    coefs[4, 2] = speed_sum

    def scale(index, k):
        return wide(scales[index, pl.ds(k, 1), :])

    def slope(g, y, cells, other):
        pulled = coefs[2, g * 2 + y] * roll_up(cells, WEST[g])
        if other is not None:
            pulled = pulled + coefs[3, g * 2 + y] * other
        return coefs[4, 2] * cells - pulled

    for d in range(2):

        def make(k, sums, d=d):
            q, s = scale(0, k), scale(1, k)
            new = []
            for gi in range(2):
                g = 2 * d + gi
                e = EDGE[g]
                energy = []
                for y in range(2):
                    cells = spectrum[k, pl.ds(g * 16 + y, 8, stride=2), :]
                    power = jnp.exp2(coefs[0, g * 2 + y] + q * coefs[1, g * 2 + y])
                    energy.append(coefs[4, y] * cells * power)
                    first = s * energy[y]
                    old = sums[(gi * 2 + y) * 3 : (gi * 2 + y) * 3 + 3]
                    new += [old[0] + energy[y], old[1] + first, old[2] + s * first]
                near[k, g] = energy[1 - e]
                far[k, g] = energy[e] - s * slope(g, e, energy[e], energy[1 - e])
            return tuple(new)

        sums = lax.fori_loop(0, freqs, make, (jnp.zeros((8, 128), F32),) * 12)
        for i in range(12):
            moments[d * 12 + i] = sums[i]

    def weigh(g):
        per = F32(1.0 / (freqs * DIRS))
        return (
            0.5 * per * cosine[g] * cosine[g],
            0.5 * per * cosine[g] * sine[g],
            0.5 * per * sine[g] * sine[g],
        )

    own = [[jnp.zeros((8, 128), F32) for _ in range(2)] for _ in range(3)]
    for d in range(2):
        direct = [jnp.zeros((8, 128), F32) for _ in range(3)]
        double = [jnp.zeros((8, 128), F32) for _ in range(3)]
        for gi in range(2):
            g = 2 * d + gi
            e = EDGE[g]
            o = 1 - e
            m_e = [moments[g * 6 + e * 3 + m] for m in range(3)]
            m_o = [moments[g * 6 + o * 3 + m] for m in range(3)]
            slope_o2 = slope(g, o, m_o[2], None)
            slope_e2 = slope(g, e, m_e[2], m_o[2])
            sum_o = m_o[0] - 2.0 * slope(g, o, m_o[1], None) + slope(g, o, slope_o2, None)
            sum_e = m_e[0] - 2.0 * slope(g, e, m_e[1], m_o[1]) + slope(g, e, slope_e2, slope_o2)
            weights = weigh(g)
            reach = abs_y[g] * (2.0 * m_e[1] - speed_sum * m_e[2] - slope_e2)
            sideways = abs_x[g] * abs_y[g] * m_e[2]
            twice = abs_y[g] * abs_y[g] * m_e[2]
            for i in range(3):
                own[i][e] = own[i][e] + weights[i] * sum_e
                own[i][o] = own[i][o] + weights[i] * sum_o
                direct[i] = direct[i] + weights[i] * reach
                double[i] = double[i] + weights[i] * twice
                edge_send[d, 8 + gi * 3 + i : 9 + gi * 3 + i, :] = reduce8(weights[i] * sideways)
        for i in range(3):
            edge_send[d, i : i + 1, :] = reduce8(direct[i])
            edge_send[d, 3 + i : 4 + i, :] = reduce8(double[i])

    def edge(d):
        return pltpu.make_async_remote_copy(
            src_ref=edge_send.at[d],
            dst_ref=edge_got.at[d],
            send_sem=edge_send_sem.at[d],
            recv_sem=edge_recv_sem.at[d],
            device_id=row_ids[d],
            device_id_type=MESH,
        )

    for d in range(2):
        edge(d).start()
    for c in range(1, last):
        for d in range(2):
            bulk(d, c).start()

    @pl.when(my_grp == 0)
    def _():
        pl.semaphore_wait(here_sem, groups - 1)
        for peer in range(1, groups):
            pl.semaphore_signal(all_sem, inc=1, device_id=(peer, my_aa), device_id_type=MESH)

    stress = [[reduce8(own[i][y]) for y in range(2)] for i in range(3)]

    for d in range(2):
        tile(d).wait_recv()
        values = others[d]
        for g in (2 * d, 2 * d + 1):
            e = EDGE[g]
            for y in range(2):
                halo[0, g * 2 + y], halo[1, g * 2 + y] = exponent(values, g, y)
            halo[2, g] = values[6 + e : 7 + e] * side[g] * abs_x[g]
            halo[3, g] = values[6 + e : 7 + e] * abs_y[g]
        for y in range(2):
            halo[4, d * 2 + y] = wide(values[6 + y : 7 + y])

    def finish(k, carry):
        q, s = scale(0, k), scale(1, k)
        for g in range(4):
            d, e = g // 2, EDGE[g]
            o = 1 - e
            base = (g % 2) * 16
            there = []
            for y in range(2):
                cells = got[d, k, pl.ds(base + y, 8, stride=2), :]
                power = jnp.exp2(halo[0, g * 2 + y] + q * halo[1, g * 2 + y])
                there.append(halo[4, d * 2 + y] * cells * power)
            pulled = halo[2, g] * roll_up(there[e], WEST[g]) + halo[3, g] * there[o]
            there_one = there[e] - s * (coefs[4, 2] * there[e] - pulled)
            start_o = near[k, g]
            one_e = far[k, g]
            one_o = start_o - s * slope(g, o, start_o, there[e])
            two_o = one_o - s * slope(g, o, one_o, there_one)
            two_e = one_e - s * slope(g, e, one_e, one_o)
            stepped[k, pl.ds(g * 16 + o, 8, stride=2), :] = two_o
            stepped[k, pl.ds(g * 16 + e, 8, stride=2), :] = two_e
        return carry

    def put(start, stop):
        where = pl.ds(start, stop - start)
        return pltpu.make_async_copy(stepped.at[where], out_hbm.at[where], out_sem)

    def finish_chunk(c):
        for d in range(2):
            bulk(d, c).wait_recv()
        lax.fori_loop(chunks[c], chunks[c + 1], finish, 0)
        put(chunks[c], chunks[c + 1]).start()

    for c in range(FIRST):
        finish_chunk(c)

    for d in range(2):
        edge(d).wait_recv()
    for copy in smalls[3:]:
        copy.wait()
    for d in range(2):
        o, e = d, 1 - d
        here = has[d] * coefs[4, o][:1]
        both = here * coefs[4, e][:1]
        sideways = edge_got[d, 8:16, :] * coefs[4, o]
        for i in range(3):
            moved = edge_got[d, i : i + 1, :]
            for gi in range(2):
                g = 2 * d + gi
                moved = moved + (side[g] * roll_up(sideways, WEST[g]))[gi * 3 + i : gi * 3 + i + 1]
            stress[i][o] = stress[i][o] + here * moved
            stress[i][e] = stress[i][e] + both * edge_got[d, 3 + i : 4 + i, :]

    target = lax.broadcasted_iota(jnp.int32, (groups * 8, 128), 0)
    place = lax.broadcasted_iota(jnp.int32, (128, 128), 0)
    summed = jnp.zeros((groups * 8, 128), F32)
    for y in range(2):
        cells = cell[y : y + 1, :]
        high = jnp.where(cells >= 128, 1, 0)
        goal = owner[y : y + 1, :] * 8 + high * 3
        spread = jnp.zeros((groups * 8, 128), F32)
        for i in range(3):
            spread = jnp.where(target == goal + i, stress[i][y], spread)
        table = jnp.where(place == cells - high * 128, 1.0, 0.0).astype(F32)
        summed = summed + lax.dot_general(
            spread,
            table,
            (((1,), (1,)), ((), ())),
            precision=lax.Precision.HIGHEST,
            preferred_element_type=F32,
        )
    parts[...] = summed.reshape(groups, 8, 128)

    @pl.when(my_grp != 0)
    def _():
        pl.semaphore_wait(all_sem, 1)

    for turn in range(1, groups):
        peer = lax.rem(my_grp + turn, groups)
        pltpu.make_async_remote_copy(
            src_ref=parts.at[peer],
            dst_ref=parts_got.at[turn - 1],
            send_sem=part_send_sem,
            recv_sem=part_recv_sem,
            device_id=(peer, my_aa),
            device_id_type=MESH,
        ).start()

    for c in range(FIRST, SECOND):
        finish_chunk(c)

    pltpu.make_async_copy(parts_got, parts_got, part_recv_sem).wait()
    summed = parts[my_grp]
    for turn in range(1, groups):
        summed = summed + parts_got[turn - 1]
    forcing[:, 0:128] = summed[0:3]
    forcing[:, 128:256] = summed[3:6]
    forcing_copy = pltpu.make_async_copy(forcing, forcing_hbm, forcing_sem)
    forcing_copy.start()

    for c in range(SECOND, last):
        finish_chunk(c)

    pltpu.make_async_copy(parts_got, parts_got, part_send_sem).wait()
    for d in range(2):
        tile(d).wait_send()
        edge(d).wait_send()
        pltpu.make_async_copy(got.at[d], got.at[d], send_sem.at[d]).wait()
    forcing_copy.wait()
    put(0, freqs).wait()


def pass_on(new, forcing, new_out, forcing_out, held, held_forcing, in_sem, out_sem):
    step = -(-held.shape[0] // PIECES)
    pairs = []
    for i in range(PIECES):
        where = pl.ds(i * step, min(step, held.shape[0] - i * step))
        pairs.append((new.at[where], held.at[where], new_out.at[where]))
    pairs.append((forcing, held_forcing, forcing_out))
    loads = [pltpu.make_async_copy(src, mid, in_sem.at[i]) for i, (src, mid, _) in enumerate(pairs)]
    stores = [pltpu.make_async_copy(mid, dst, out_sem.at[i]) for i, (_, mid, dst) in enumerate(pairs)]
    for copy in loads:
        copy.start()
    for load, store in zip(loads, stores):
        load.wait()
        store.start()
    for copy in stores:
        copy.wait()


def on_device(groups, spectrum, friction, wind_dir, wet, owner, cell):
    comps, rows, width = spectrum.shape
    freqs = comps // DIRS
    chunks = CHUNKS if CHUNKS[-1] == freqs else tuple(range(0, freqs + 1, 2))
    last = len(chunks) - 1
    anywhere = pl.BlockSpec(memory_space=pl.ANY)
    dma = pltpu.SemaphoreType.DMA
    results = (
        jax.ShapeDtypeStruct((freqs, 2 * DIRS, width), F32),
        jax.ShapeDtypeStruct((3, 256), F32),
    )
    vmem = pltpu.VMEM
    new, forcing = pl.pallas_call(
        functools.partial(kernel, chunks),
        out_shape=results,
        in_specs=[anywhere] * 6,
        out_specs=(anywhere, anywhere),
        scratch_shapes=[
            vmem((freqs, 2 * DIRS, width), F32),
            vmem((rows, width), F32),
            vmem((rows, width), F32),
            vmem((8, width), jnp.int32),
            vmem((rows, width), jnp.int32),
            vmem((rows, width), jnp.int32),
            vmem((freqs, 2 * DIRS, width), F32),
            vmem((2, freqs, DIRS, width), F32),
            vmem((freqs, 4, 8, width), F32),
            vmem((freqs, 4, 8, width), F32),
            vmem((8, width), F32),
            vmem((2, 8, width), F32),
            vmem((5, 8, 8, width), F32),
            vmem((5, 8, 8, width), F32),
            vmem((2, (freqs + 7) // 8 * 8, width), F32),
            vmem((24, 8, width), F32),
            vmem((2, 16, width), F32),
            vmem((2, 16, width), F32),
            vmem((groups, 8, width), F32),
            vmem((groups - 1, 8, width), F32),
            vmem((3, 256), F32),
            dma((2,)),
            dma((5,)),
            dma((2,)),
            dma((2, last)),
            dma((2,)),
            dma((2,)),
            dma((2,)),
            dma((2,)),
            dma,
            dma,
            dma,
            dma,
            pltpu.SemaphoreType.REGULAR,
            pltpu.SemaphoreType.REGULAR,
        ],
        compiler_params=pltpu.CompilerParams(
            collective_id=0, has_side_effects=True, vmem_limit_bytes=LIMIT
        ),
    )(
        spectrum.reshape(freqs, 2 * DIRS, width),
        friction,
        wind_dir,
        wet,
        owner.reshape(rows, width),
        cell,
    )
    new, forcing = pl.pallas_call(
        pass_on,
        out_shape=results,
        in_specs=[anywhere] * 2,
        out_specs=(anywhere, anywhere),
        scratch_shapes=[
            vmem((freqs, 2 * DIRS, width), F32),
            vmem((3, 256), F32),
            dma((PIECES + 1,)),
            dma((PIECES + 1,)),
        ],
        compiler_params=pltpu.CompilerParams(vmem_limit_bytes=LIMIT),
    )(new, forcing)
    return new.reshape(comps, rows, width), forcing


def solution(mesh):
    placed = (
        P(None, ("grp", "aa"), None),
        P(("grp", "aa"), None),
        P(("grp", "aa"), None),
        P("grp", None),
        P(("grp", "aa"), None),
        P(("grp", "aa"), None),
    )
    return jax.shard_map(
        functools.partial(on_device, mesh.shape["grp"]),
        mesh=mesh,
        in_specs=placed,
        out_specs=(P(None, ("grp", "aa"), None), P(None, ("grp", "aa"))),
        check_vma=False,
    )
```

```python
import functools
import math

import jax
import jax.numpy as jnp
from jax import lax
from jax.experimental import pallas as pl
from jax.experimental.pallas import tpu as pltpu
from jax.sharding import PartitionSpec as P

MESH = pl.DeviceIdType.MESH
DIRS = 32
COURANT = 0.7
LOG2E = math.log2(math.e)
CHUNKS = (0, 15, 30, 45, 50)
FIRST, SECOND = 1, 3
PIECES = 4
LIMIT = 60 * 1024 * 1024
F32 = jnp.float32

EDGE = (1, 1, 0, 0)
WEST = (True, False, False, True)


def roll_up(cells, west):
    return pltpu.roll(cells, 1 if west else 127, 1)


def wide(cells):
    return jnp.broadcast_to(cells, (8, 128))


def reduce8(cells):
    return jnp.sum(cells, axis=0, keepdims=True)


def kernel(
    chunks,
    spectrum_hbm,
    friction_hbm,
    wind_hbm,
    wet_hbm,
    owner_hbm,
    cell_hbm,
    out_hbm,
    forcing_hbm,
    spectrum,
    friction,
    wind,
    wet,
    owner,
    cell,
    stepped,
    got,
    near,
    far,
    mine,
    others,
    coefs,
    halo,
    scales,
    moments,
    edge_send,
    edge_got,
    parts,
    parts_got,
    forcing,
    load_sem,
    small_sem,
    send_sem,
    recv_sem,
    tile_send_sem,
    tile_recv_sem,
    edge_send_sem,
    edge_recv_sem,
    part_send_sem,
    part_recv_sem,
    out_sem,
    forcing_sem,
    here_sem,
    all_sem,
):
    freqs = spectrum.shape[0]
    groups, column = lax.axis_size("grp"), lax.axis_size("aa")
    my_grp, my_aa = lax.axis_index("grp"), lax.axis_index("aa")
    devices = groups * column
    me = my_grp * column + my_aa
    after = lax.rem(me + 1, devices)
    before = lax.rem(me + devices - 1, devices)
    row_ids = ((after // column, lax.rem(after, column)), (before // column, lax.rem(before, column)))
    last = len(chunks) - 1

    barrier = pltpu.get_barrier_semaphore()
    for other in row_ids:
        pl.semaphore_signal(barrier, inc=1, device_id=other, device_id_type=MESH)

    @pl.when(my_grp == 0)
    def _():
        for peer in range(1, groups):
            pl.semaphore_signal(barrier, inc=1, device_id=(peer, my_aa), device_id_type=MESH)

    half = freqs // 2
    loads = [
        pltpu.make_async_copy(spectrum_hbm.at[pl.ds(i * half, half)], spectrum.at[pl.ds(i * half, half)], load_sem.at[i])
        for i in range(2)
    ]
    wet_start = pl.multiple_of((2 * my_aa) // 8 * 8, 8)
    smalls = [
        pltpu.make_async_copy(friction_hbm, friction, small_sem.at[0]),
        pltpu.make_async_copy(wind_hbm, wind, small_sem.at[1]),
        pltpu.make_async_copy(wet_hbm.at[pl.ds(wet_start, 8)], wet, small_sem.at[2]),
        pltpu.make_async_copy(owner_hbm, owner, small_sem.at[3]),
        pltpu.make_async_copy(cell_hbm, cell, small_sem.at[4]),
    ]
    for copy in smalls[:3] + loads + smalls[3:]:
        copy.start()
    pl.semaphore_wait(barrier, jnp.where(my_grp == 0, 2, 3))

    def bulk(d, c):
        where = pl.ds(chunks[c], chunks[c + 1] - chunks[c])
        return pltpu.make_async_remote_copy(
            src_ref=spectrum_hbm.at[where, pl.ds(32 * d, 32)],
            dst_ref=got.at[d, where],
            send_sem=send_sem.at[d],
            recv_sem=recv_sem.at[d, c],
            device_id=row_ids[d],
            device_id_type=MESH,
        )

    for d in range(2):
        bulk(d, 0).start()

    @pl.when(my_grp != 0)
    def _():
        pl.semaphore_signal(here_sem, inc=1, device_id=(0, my_aa), device_id_type=MESH)

    lane = lax.broadcasted_iota(jnp.int32, (8, 128), 1)
    place8 = lax.broadcasted_iota(jnp.int32, (8, 128), 0)
    cos0 = jnp.full((8, 128), 1.0, F32)
    sin0 = jnp.full((8, 128), 0.0, F32)
    for j in range(1, 8):
        cos0 = jnp.where(place8 == j, F32(math.cos(2.0 * math.pi * j / DIRS)), cos0)
        sin0 = jnp.where(place8 == j, F32(math.sin(2.0 * math.pi * j / DIRS)), sin0)
    cosine = (cos0, -sin0, -cos0, sin0)
    sine = (sin0, cos0, -sin0, -cos0)
    abs_x = [COURANT * c for c in (cos0, sin0, cos0, sin0)]
    abs_y = [COURANT * c for c in (sin0, cos0, sin0, cos0)]
    speed_sum = COURANT * (cos0 + sin0)
    side = [jnp.where(lane != 0, 1.0, 0.0) if west else jnp.where(lane != 127, 1.0, 0.0) for west in WEST]
    number = lax.broadcasted_iota(jnp.int32, scales.shape[1:], 0).astype(F32) * F32(1.0 / max(freqs - 1, 1))
    scales[0] = number
    scales[1] = jnp.exp2(-number)
    edge_send[...] = jnp.zeros_like(edge_send)
    has = [jnp.where(me > 0, 1.0, 0.0).astype(F32), jnp.where(me < devices - 1, 1.0, 0.0).astype(F32)]

    for copy in smalls[:3]:
        copy.wait()
    grow = 0.4 * friction[...]
    mine[0:2, :] = grow * jnp.cos(wind[...])
    mine[2:4, :] = grow * jnp.sin(wind[...])
    wet_row = lax.rem(2 * my_aa, 8)
    for y in range(2):
        mine[6 + y : 7 + y, :] = wet[pl.ds(wet_row + y, 1), :].astype(F32)

    def add(k, acc):
        return acc + jnp.sum(spectrum[k].reshape(8, 8, 128), axis=0)

    acc = jnp.zeros((8, 128), F32)
    for i in range(2):
        loads[i].wait()
        acc = lax.fori_loop(i * half, (i + 1) * half, add, acc)
    for y in range(2):
        total = reduce8(jnp.where(lax.rem(place8, 2) == y, acc, 0.0)) / F32(freqs * DIRS)
        mine[4 + y : 5 + y, :] = total / (1.0 + total)

    def tile(d):
        return pltpu.make_async_remote_copy(
            src_ref=mine,
            dst_ref=others.at[d],
            send_sem=tile_send_sem.at[d],
            recv_sem=tile_recv_sem.at[d],
            device_id=row_ids[d],
            device_id_type=MESH,
        )

    for d in range(2):
        tile(d).start()

    def exponent(values, g, y):
        growth = jnp.maximum(cosine[g] * values[0 + y : 1 + y] + sine[g] * values[2 + y : 3 + y], 0.0)
        damp = values[4 + y : 5 + y]
        return LOG2E * (0.5 * growth - 0.15 * damp), LOG2E * (growth - 0.6 * damp)

    values = mine[...]
    for g in range(4):
        for y in range(2):
            coefs[0, g * 2 + y], coefs[1, g * 2 + y] = exponent(values, g, y)
            coefs[2, g * 2 + y] = values[6 + y : 7 + y] * side[g] * abs_x[g]
            pull = values[6 + y : 7 + y] * abs_y[g]
            coefs[3, g * 2 + y] = pull if y == EDGE[g] else pull * has[g // 2]
    for y in range(2):
        coefs[4, y] = wide(values[6 + y : 7 + y])
    coefs[4, 2] = speed_sum

    def scale(index, k):
        return wide(scales[index, pl.ds(k, 1), :])

    def slope(g, y, cells, other):
        pulled = coefs[2, g * 2 + y] * roll_up(cells, WEST[g])
        if other is not None:
            pulled = pulled + coefs[3, g * 2 + y] * other
        return coefs[4, 2] * cells - pulled

    for d in range(2):

        def make(k, sums, d=d):
            q, s = scale(0, k), scale(1, k)
            new = []
            for gi in range(2):
                g = 2 * d + gi
                e = EDGE[g]
                energy = []
                for y in range(2):
                    cells = spectrum[k, pl.ds(g * 16 + y, 8, stride=2), :]
                    power = jnp.exp2(coefs[0, g * 2 + y] + q * coefs[1, g * 2 + y])
                    energy.append(coefs[4, y] * cells * power)
                    first = s * energy[y]
                    old = sums[(gi * 2 + y) * 3 : (gi * 2 + y) * 3 + 3]
                    new += [old[0] + energy[y], old[1] + first, old[2] + s * first]
                near[k, g] = energy[1 - e]
                far[k, g] = energy[e] - s * slope(g, e, energy[e], energy[1 - e])
            return tuple(new)

        sums = lax.fori_loop(0, freqs, make, (jnp.zeros((8, 128), F32),) * 12, unroll=10)
        for i in range(12):
            moments[d * 12 + i] = sums[i]

    def weigh(g):
        per = F32(1.0 / (freqs * DIRS))
        return (
            0.5 * per * cosine[g] * cosine[g],
            0.5 * per * cosine[g] * sine[g],
            0.5 * per * sine[g] * sine[g],
        )

    own = [[jnp.zeros((8, 128), F32) for _ in range(2)] for _ in range(3)]
    for d in range(2):
        direct = [jnp.zeros((8, 128), F32) for _ in range(3)]
        double = [jnp.zeros((8, 128), F32) for _ in range(3)]
        for gi in range(2):
            g = 2 * d + gi
            e = EDGE[g]
            o = 1 - e
            m_e = [moments[g * 6 + e * 3 + m] for m in range(3)]
            m_o = [moments[g * 6 + o * 3 + m] for m in range(3)]
            slope_o2 = slope(g, o, m_o[2], None)
            slope_e2 = slope(g, e, m_e[2], m_o[2])
            sum_o = m_o[0] - 2.0 * slope(g, o, m_o[1], None) + slope(g, o, slope_o2, None)
            sum_e = m_e[0] - 2.0 * slope(g, e, m_e[1], m_o[1]) + slope(g, e, slope_e2, slope_o2)
            weights = weigh(g)
            reach = abs_y[g] * (2.0 * m_e[1] - speed_sum * m_e[2] - slope_e2)
            sideways = abs_x[g] * abs_y[g] * m_e[2]
            twice = abs_y[g] * abs_y[g] * m_e[2]
            for i in range(3):
                own[i][e] = own[i][e] + weights[i] * sum_e
                own[i][o] = own[i][o] + weights[i] * sum_o
                direct[i] = direct[i] + weights[i] * reach
                double[i] = double[i] + weights[i] * twice
                edge_send[d, 8 + gi * 3 + i : 9 + gi * 3 + i, :] = reduce8(weights[i] * sideways)
        for i in range(3):
            edge_send[d, i : i + 1, :] = reduce8(direct[i])
            edge_send[d, 3 + i : 4 + i, :] = reduce8(double[i])

    def edge(d):
        return pltpu.make_async_remote_copy(
            src_ref=edge_send.at[d],
            dst_ref=edge_got.at[d],
            send_sem=edge_send_sem.at[d],
            recv_sem=edge_recv_sem.at[d],
            device_id=row_ids[d],
            device_id_type=MESH,
        )

    for d in range(2):
        edge(d).start()
    for c in range(1, last):
        for d in range(2):
            bulk(d, c).start()

    @pl.when(my_grp == 0)
    def _():
        pl.semaphore_wait(here_sem, groups - 1)
        for peer in range(1, groups):
            pl.semaphore_signal(all_sem, inc=1, device_id=(peer, my_aa), device_id_type=MESH)

    stress = [[reduce8(own[i][y]) for y in range(2)] for i in range(3)]

    for d in range(2):
        tile(d).wait_recv()
        values = others[d]
        for g in (2 * d, 2 * d + 1):
            e = EDGE[g]
            for y in range(2):
                halo[0, g * 2 + y], halo[1, g * 2 + y] = exponent(values, g, y)
            halo[2, g] = values[6 + e : 7 + e] * side[g] * abs_x[g]
            halo[3, g] = values[6 + e : 7 + e] * abs_y[g]
        for y in range(2):
            halo[4, d * 2 + y] = wide(values[6 + y : 7 + y])

    def finish(k, carry):
        q, s = scale(0, k), scale(1, k)
        for g in range(4):
            d, e = g // 2, EDGE[g]
            o = 1 - e
            base = (g % 2) * 16
            there = []
            for y in range(2):
                cells = got[d, k, pl.ds(base + y, 8, stride=2), :]
                power = jnp.exp2(halo[0, g * 2 + y] + q * halo[1, g * 2 + y])
                there.append(halo[4, d * 2 + y] * cells * power)
            pulled = halo[2, g] * roll_up(there[e], WEST[g]) + halo[3, g] * there[o]
            there_one = there[e] - s * (coefs[4, 2] * there[e] - pulled)
            start_o = near[k, g]
            one_e = far[k, g]
            one_o = start_o - s * slope(g, o, start_o, there[e])
            two_o = one_o - s * slope(g, o, one_o, there_one)
            two_e = one_e - s * slope(g, e, one_e, one_o)
            stepped[k, pl.ds(g * 16 + o, 8, stride=2), :] = two_o
            stepped[k, pl.ds(g * 16 + e, 8, stride=2), :] = two_e
        return carry

    def put(start, stop):
        where = pl.ds(start, stop - start)
        return pltpu.make_async_copy(stepped.at[where], out_hbm.at[where], out_sem)

    def finish_chunk(c):
        for d in range(2):
            bulk(d, c).wait_recv()
        lax.fori_loop(chunks[c], chunks[c + 1], finish, 0, unroll=5)
        put(chunks[c], chunks[c + 1]).start()

    for c in range(FIRST):
        finish_chunk(c)

    for d in range(2):
        edge(d).wait_recv()
    for copy in smalls[3:]:
        copy.wait()
    for d in range(2):
        o, e = d, 1 - d
        here = has[d] * coefs[4, o][:1]
        both = here * coefs[4, e][:1]
        sideways = edge_got[d, 8:16, :] * coefs[4, o]
        for i in range(3):
            moved = edge_got[d, i : i + 1, :]
            for gi in range(2):
                g = 2 * d + gi
                moved = moved + (side[g] * roll_up(sideways, WEST[g]))[gi * 3 + i : gi * 3 + i + 1]
            stress[i][o] = stress[i][o] + here * moved
            stress[i][e] = stress[i][e] + both * edge_got[d, 3 + i : 4 + i, :]

    target = lax.broadcasted_iota(jnp.int32, (groups * 8, 128), 0)
    place = lax.broadcasted_iota(jnp.int32, (128, 128), 0)
    summed = jnp.zeros((groups * 8, 128), F32)
    for y in range(2):
        cells = cell[y : y + 1, :]
        high = jnp.where(cells >= 128, 1, 0)
        goal = owner[y : y + 1, :] * 8 + high * 3
        spread = jnp.zeros((groups * 8, 128), F32)
        for i in range(3):
            spread = jnp.where(target == goal + i, stress[i][y], spread)
        table = jnp.where(place == cells - high * 128, 1.0, 0.0).astype(F32)
        summed = summed + lax.dot_general(
            spread,
            table,
            (((1,), (1,)), ((), ())),
            precision=lax.Precision.HIGHEST,
            preferred_element_type=F32,
        )
    parts[...] = summed.reshape(groups, 8, 128)

    @pl.when(my_grp != 0)
    def _():
        pl.semaphore_wait(all_sem, 1)

    for turn in range(1, groups):
        peer = lax.rem(my_grp + turn, groups)
        pltpu.make_async_remote_copy(
            src_ref=parts.at[peer],
            dst_ref=parts_got.at[turn - 1],
            send_sem=part_send_sem,
            recv_sem=part_recv_sem,
            device_id=(peer, my_aa),
            device_id_type=MESH,
        ).start()

    for c in range(FIRST, SECOND):
        finish_chunk(c)

    pltpu.make_async_copy(parts_got, parts_got, part_recv_sem).wait()
    summed = parts[my_grp]
    for turn in range(1, groups):
        summed = summed + parts_got[turn - 1]
    forcing[:, 0:128] = summed[0:3]
    forcing[:, 128:256] = summed[3:6]
    forcing_copy = pltpu.make_async_copy(forcing, forcing_hbm, forcing_sem)
    forcing_copy.start()

    for c in range(SECOND, last):
        finish_chunk(c)

    pltpu.make_async_copy(parts_got, parts_got, part_send_sem).wait()
    for d in range(2):
        tile(d).wait_send()
        edge(d).wait_send()
        pltpu.make_async_copy(got.at[d], got.at[d], send_sem.at[d]).wait()
    forcing_copy.wait()
    put(0, freqs).wait()


def pass_on(new, forcing, new_out, forcing_out, held, held_forcing, in_sem, out_sem):
    step = -(-held.shape[0] // PIECES)
    pairs = []
    for i in range(PIECES):
        where = pl.ds(i * step, min(step, held.shape[0] - i * step))
        pairs.append((new.at[where], held.at[where], new_out.at[where]))
    pairs.append((forcing, held_forcing, forcing_out))
    loads = [pltpu.make_async_copy(src, mid, in_sem.at[i]) for i, (src, mid, _) in enumerate(pairs)]
    stores = [pltpu.make_async_copy(mid, dst, out_sem.at[i]) for i, (_, mid, dst) in enumerate(pairs)]
    for copy in loads:
        copy.start()
    for load, store in zip(loads, stores):
        load.wait()
        store.start()
    for copy in stores:
        copy.wait()


def on_device(groups, spectrum, friction, wind_dir, wet, owner, cell):
    comps, rows, width = spectrum.shape
    freqs = comps // DIRS
    chunks = CHUNKS if CHUNKS[-1] == freqs else tuple(range(0, freqs + 1, 2))
    last = len(chunks) - 1
    anywhere = pl.BlockSpec(memory_space=pl.ANY)
    dma = pltpu.SemaphoreType.DMA
    results = (
        jax.ShapeDtypeStruct((freqs, 2 * DIRS, width), F32),
        jax.ShapeDtypeStruct((3, 256), F32),
    )
    vmem = pltpu.VMEM
    new, forcing = pl.pallas_call(
        functools.partial(kernel, chunks),
        out_shape=results,
        in_specs=[anywhere] * 6,
        out_specs=(anywhere, anywhere),
        scratch_shapes=[
            vmem((freqs, 2 * DIRS, width), F32),
            vmem((rows, width), F32),
            vmem((rows, width), F32),
            vmem((8, width), jnp.int32),
            vmem((rows, width), jnp.int32),
            vmem((rows, width), jnp.int32),
            vmem((freqs, 2 * DIRS, width), F32),
            vmem((2, freqs, DIRS, width), F32),
            vmem((freqs, 4, 8, width), F32),
            vmem((freqs, 4, 8, width), F32),
            vmem((8, width), F32),
            vmem((2, 8, width), F32),
            vmem((5, 8, 8, width), F32),
            vmem((5, 8, 8, width), F32),
            vmem((2, (freqs + 7) // 8 * 8, width), F32),
            vmem((24, 8, width), F32),
            vmem((2, 16, width), F32),
            vmem((2, 16, width), F32),
            vmem((groups, 8, width), F32),
            vmem((groups - 1, 8, width), F32),
            vmem((3, 256), F32),
            dma((2,)),
            dma((5,)),
            dma((2,)),
            dma((2, last)),
            dma((2,)),
            dma((2,)),
            dma((2,)),
            dma((2,)),
            dma,
            dma,
            dma,
            dma,
            pltpu.SemaphoreType.REGULAR,
            pltpu.SemaphoreType.REGULAR,
        ],
        compiler_params=pltpu.CompilerParams(
            collective_id=0, has_side_effects=True, vmem_limit_bytes=LIMIT
        ),
    )(
        spectrum.reshape(freqs, 2 * DIRS, width),
        friction,
        wind_dir,
        wet,
        owner.reshape(rows, width),
        cell,
    )
    new, forcing = pl.pallas_call(
        pass_on,
        out_shape=results,
        in_specs=[anywhere] * 2,
        out_specs=(anywhere, anywhere),
        scratch_shapes=[
            vmem((freqs, 2 * DIRS, width), F32),
            vmem((3, 256), F32),
            dma((PIECES + 1,)),
            dma((PIECES + 1,)),
        ],
        compiler_params=pltpu.CompilerParams(vmem_limit_bytes=LIMIT),
    )(new, forcing)
    return new.reshape(comps, rows, width), forcing


def solution(mesh):
    placed = (
        P(None, ("grp", "aa"), None),
        P(("grp", "aa"), None),
        P(("grp", "aa"), None),
        P("grp", None),
        P(("grp", "aa"), None),
        P(("grp", "aa"), None),
    )
    return jax.shard_map(
        functools.partial(on_device, mesh.shape["grp"]),
        mesh=mesh,
        in_specs=placed,
        out_specs=(P(None, ("grp", "aa"), None), P(None, ("grp", "aa"))),
        check_vma=False,
    )
```

```python
import functools
import math

import jax
import jax.numpy as jnp
from jax import lax
from jax.experimental import pallas as pl
from jax.experimental.pallas import tpu as pltpu
from jax.sharding import PartitionSpec as P

MESH = pl.DeviceIdType.MESH
DIRS = 32
COURANT = 0.7
LOG2E = math.log2(math.e)
CHUNKS = (0, 15, 30, 45, 48, 50)
FIRST, SECOND = 1, 3
PIECES = 4
LIMIT = 60 * 1024 * 1024
F32 = jnp.float32

EDGE = (1, 1, 0, 0)
SKIP = (2, 0)
WEST = (True, False, False, True)


def roll_up(cells, west):
    return pltpu.roll(cells, 1 if west else 127, 1)


def wide(cells):
    return jnp.broadcast_to(cells, (8, 128))


def reduce8(cells):
    return jnp.sum(cells, axis=0, keepdims=True)


def kernel(
    chunks,
    spectrum_hbm,
    friction_hbm,
    wind_hbm,
    wet_hbm,
    owner_hbm,
    cell_hbm,
    stepped,
    forcing,
    spectrum,
    friction,
    wind,
    wet,
    owner,
    cell,
    got,
    near,
    far,
    mine,
    others,
    coefs,
    halo,
    scales,
    moments,
    edge_send,
    edge_got,
    parts,
    parts_got,
    load_sem,
    small_sem,
    send_sem,
    recv_sem,
    tile_send_sem,
    tile_recv_sem,
    edge_send_sem,
    edge_recv_sem,
    part_send_sem,
    part_recv_sem,
    here_sem,
    all_sem,
):
    freqs = spectrum.shape[0]
    groups, column = lax.axis_size("grp"), lax.axis_size("aa")
    my_grp, my_aa = lax.axis_index("grp"), lax.axis_index("aa")
    devices = groups * column
    me = my_grp * column + my_aa
    after = lax.rem(me + 1, devices)
    before = lax.rem(me + devices - 1, devices)
    row_ids = ((after // column, lax.rem(after, column)), (before // column, lax.rem(before, column)))
    last = len(chunks) - 1

    barrier = pltpu.get_barrier_semaphore()
    got[0, :, 0 : SKIP[0], :] = jnp.zeros((freqs, SKIP[0], 128), F32)
    for other in row_ids:
        pl.semaphore_signal(barrier, inc=1, device_id=other, device_id_type=MESH)

    @pl.when(my_grp == 0)
    def _():
        for peer in range(1, groups):
            pl.semaphore_signal(barrier, inc=1, device_id=(peer, my_aa), device_id_type=MESH)

    half = freqs // 2
    loads = [
        pltpu.make_async_copy(spectrum_hbm.at[pl.ds(i * half, half)], spectrum.at[pl.ds(i * half, half)], load_sem.at[i])
        for i in range(2)
    ]
    wet_start = pl.multiple_of((2 * my_aa) // 8 * 8, 8)
    smalls = [
        pltpu.make_async_copy(friction_hbm, friction, small_sem.at[0]),
        pltpu.make_async_copy(wind_hbm, wind, small_sem.at[1]),
        pltpu.make_async_copy(wet_hbm.at[pl.ds(wet_start, 8)], wet, small_sem.at[2]),
        pltpu.make_async_copy(owner_hbm, owner, small_sem.at[3]),
        pltpu.make_async_copy(cell_hbm, cell, small_sem.at[4]),
    ]
    for copy in smalls[:3] + loads + smalls[3:]:
        copy.start()
    pl.semaphore_wait(barrier, jnp.where(my_grp == 0, 2, 3))

    def bulk(d, c):
        where = pl.ds(chunks[c], chunks[c + 1] - chunks[c])
        first = SKIP[d]
        return pltpu.make_async_remote_copy(
            src_ref=spectrum_hbm.at[where, pl.ds(32 * d + first, 32 - first)],
            dst_ref=got.at[d, where, pl.ds(first, 32 - first)],
            send_sem=send_sem.at[d],
            recv_sem=recv_sem.at[d, c],
            device_id=row_ids[d],
            device_id_type=MESH,
        )

    for d in range(2):
        bulk(d, 0).start()

    @pl.when(my_grp != 0)
    def _():
        pl.semaphore_signal(here_sem, inc=1, device_id=(0, my_aa), device_id_type=MESH)

    lane = lax.broadcasted_iota(jnp.int32, (8, 128), 1)
    place8 = lax.broadcasted_iota(jnp.int32, (8, 128), 0)
    cos0 = jnp.full((8, 128), 1.0, F32)
    sin0 = jnp.full((8, 128), 0.0, F32)
    for j in range(1, 8):
        cos0 = jnp.where(place8 == j, F32(math.cos(2.0 * math.pi * j / DIRS)), cos0)
        sin0 = jnp.where(place8 == j, F32(math.sin(2.0 * math.pi * j / DIRS)), sin0)
    cosine = (cos0, -sin0, -cos0, sin0)
    sine = (sin0, cos0, -sin0, -cos0)
    abs_x = [COURANT * c for c in (cos0, sin0, cos0, sin0)]
    abs_y = [COURANT * c for c in (sin0, cos0, sin0, cos0)]
    speed_sum = COURANT * (cos0 + sin0)
    side = [jnp.where(lane != 0, 1.0, 0.0) if west else jnp.where(lane != 127, 1.0, 0.0) for west in WEST]
    number = lax.broadcasted_iota(jnp.int32, scales.shape[1:], 0).astype(F32) * F32(1.0 / max(freqs - 1, 1))
    scales[0] = number
    scales[1] = jnp.exp2(-number)
    edge_send[...] = jnp.zeros_like(edge_send)
    has = [jnp.where(me > 0, 1.0, 0.0).astype(F32), jnp.where(me < devices - 1, 1.0, 0.0).astype(F32)]

    for copy in smalls[:3]:
        copy.wait()
    grow = 0.4 * friction[...]
    mine[0:2, :] = grow * jnp.cos(wind[...])
    mine[2:4, :] = grow * jnp.sin(wind[...])
    wet_row = lax.rem(2 * my_aa, 8)
    for y in range(2):
        mine[6 + y : 7 + y, :] = wet[pl.ds(wet_row + y, 1), :].astype(F32)

    def add(k, acc):
        return acc + jnp.sum(spectrum[k].reshape(8, 8, 128), axis=0)

    acc = jnp.zeros((8, 128), F32)
    for i in range(2):
        loads[i].wait()
        acc = lax.fori_loop(i * half, (i + 1) * half, add, acc)
    for y in range(2):
        total = reduce8(jnp.where(lax.rem(place8, 2) == y, acc, 0.0)) / F32(freqs * DIRS)
        mine[4 + y : 5 + y, :] = total / (1.0 + total)

    def tile(d):
        return pltpu.make_async_remote_copy(
            src_ref=mine,
            dst_ref=others.at[d],
            send_sem=tile_send_sem.at[d],
            recv_sem=tile_recv_sem.at[d],
            device_id=row_ids[d],
            device_id_type=MESH,
        )

    for d in range(2):
        tile(d).start()

    def exponent(values, g, y):
        growth = jnp.maximum(cosine[g] * values[0 + y : 1 + y] + sine[g] * values[2 + y : 3 + y], 0.0)
        damp = values[4 + y : 5 + y]
        return LOG2E * (0.5 * growth - 0.15 * damp), LOG2E * (growth - 0.6 * damp)

    values = mine[...]
    for g in range(4):
        for y in range(2):
            coefs[0, g * 2 + y], coefs[1, g * 2 + y] = exponent(values, g, y)
            coefs[2, g * 2 + y] = values[6 + y : 7 + y] * side[g] * abs_x[g]
            pull = values[6 + y : 7 + y] * abs_y[g]
            coefs[3, g * 2 + y] = pull if y == EDGE[g] else pull * has[g // 2]
    for y in range(2):
        coefs[4, y] = wide(values[6 + y : 7 + y])
    coefs[4, 2] = speed_sum

    def scale(index, k):
        return wide(scales[index, pl.ds(k, 1), :])

    def slope(g, y, cells, other):
        pulled = coefs[2, g * 2 + y] * roll_up(cells, WEST[g])
        if other is not None:
            pulled = pulled + coefs[3, g * 2 + y] * other
        return coefs[4, 2] * cells - pulled

    for d in range(2):

        def make(k, sums, d=d):
            q, s = scale(0, k), scale(1, k)
            new = []
            for gi in range(2):
                g = 2 * d + gi
                e = EDGE[g]
                energy = []
                for y in range(2):
                    cells = spectrum[k, pl.ds(g * 16 + y, 8, stride=2), :]
                    power = jnp.exp2(coefs[0, g * 2 + y] + q * coefs[1, g * 2 + y])
                    energy.append(coefs[4, y] * cells * power)
                    first = s * energy[y]
                    old = sums[(gi * 2 + y) * 3 : (gi * 2 + y) * 3 + 3]
                    new += [old[0] + energy[y], old[1] + first, old[2] + s * first]
                near[k, g] = energy[1 - e]
                far[k, g] = energy[e] - s * slope(g, e, energy[e], energy[1 - e])
            return tuple(new)

        sums = lax.fori_loop(0, freqs, make, (jnp.zeros((8, 128), F32),) * 12, unroll=10)
        for i in range(12):
            moments[d * 12 + i] = sums[i]

    def weigh(g):
        per = F32(1.0 / (freqs * DIRS))
        return (
            0.5 * per * cosine[g] * cosine[g],
            0.5 * per * cosine[g] * sine[g],
            0.5 * per * sine[g] * sine[g],
        )

    own = [[jnp.zeros((8, 128), F32) for _ in range(2)] for _ in range(3)]
    for d in range(2):
        direct = [jnp.zeros((8, 128), F32) for _ in range(3)]
        double = [jnp.zeros((8, 128), F32) for _ in range(3)]
        for gi in range(2):
            g = 2 * d + gi
            e = EDGE[g]
            o = 1 - e
            m_e = [moments[g * 6 + e * 3 + m] for m in range(3)]
            m_o = [moments[g * 6 + o * 3 + m] for m in range(3)]
            slope_o2 = slope(g, o, m_o[2], None)
            slope_e2 = slope(g, e, m_e[2], m_o[2])
            sum_o = m_o[0] - 2.0 * slope(g, o, m_o[1], None) + slope(g, o, slope_o2, None)
            sum_e = m_e[0] - 2.0 * slope(g, e, m_e[1], m_o[1]) + slope(g, e, slope_e2, slope_o2)
            weights = weigh(g)
            reach = abs_y[g] * (2.0 * m_e[1] - speed_sum * m_e[2] - slope_e2)
            sideways = abs_x[g] * abs_y[g] * m_e[2]
            twice = abs_y[g] * abs_y[g] * m_e[2]
            for i in range(3):
                own[i][e] = own[i][e] + weights[i] * sum_e
                own[i][o] = own[i][o] + weights[i] * sum_o
                direct[i] = direct[i] + weights[i] * reach
                double[i] = double[i] + weights[i] * twice
                edge_send[d, 8 + gi * 3 + i : 9 + gi * 3 + i, :] = reduce8(weights[i] * sideways)
        for i in range(3):
            edge_send[d, i : i + 1, :] = reduce8(direct[i])
            edge_send[d, 3 + i : 4 + i, :] = reduce8(double[i])

    def edge(d):
        return pltpu.make_async_remote_copy(
            src_ref=edge_send.at[d],
            dst_ref=edge_got.at[d],
            send_sem=edge_send_sem.at[d],
            recv_sem=edge_recv_sem.at[d],
            device_id=row_ids[d],
            device_id_type=MESH,
        )

    for d in range(2):
        edge(d).start()
    for c in range(1, last):
        for d in range(2):
            bulk(d, c).start()

    @pl.when(my_grp == 0)
    def _():
        pl.semaphore_wait(here_sem, groups - 1)
        for peer in range(1, groups):
            pl.semaphore_signal(all_sem, inc=1, device_id=(peer, my_aa), device_id_type=MESH)

    stress = [[reduce8(own[i][y]) for y in range(2)] for i in range(3)]

    for d in range(2):
        tile(d).wait_recv()
        values = others[d]
        for g in (2 * d, 2 * d + 1):
            e = EDGE[g]
            for y in range(2):
                halo[0, g * 2 + y], halo[1, g * 2 + y] = exponent(values, g, y)
            halo[2, g] = values[6 + e : 7 + e] * side[g] * abs_x[g]
            halo[3, g] = values[6 + e : 7 + e] * abs_y[g]
        for y in range(2):
            halo[4, d * 2 + y] = wide(values[6 + y : 7 + y])

    def finish(k, carry):
        q, s = scale(0, k), scale(1, k)
        for g in range(4):
            d, e = g // 2, EDGE[g]
            o = 1 - e
            base = (g % 2) * 16
            there = []
            for y in range(2):
                cells = got[d, k, pl.ds(base + y, 8, stride=2), :]
                power = jnp.exp2(halo[0, g * 2 + y] + q * halo[1, g * 2 + y])
                there.append(halo[4, d * 2 + y] * cells * power)
            pulled = halo[2, g] * roll_up(there[e], WEST[g]) + halo[3, g] * there[o]
            there_one = there[e] - s * (coefs[4, 2] * there[e] - pulled)
            start_o = near[k, g]
            one_e = far[k, g]
            one_o = start_o - s * slope(g, o, start_o, there[e])
            two_o = one_o - s * slope(g, o, one_o, there_one)
            two_e = one_e - s * slope(g, e, one_e, one_o)
            stepped[k, pl.ds(g * 16 + o, 8, stride=2), :] = two_o
            stepped[k, pl.ds(g * 16 + e, 8, stride=2), :] = two_e
        return carry

    def finish_chunk(c):
        for d in range(2):
            bulk(d, c).wait_recv()
        lax.fori_loop(chunks[c], chunks[c + 1], finish, 0, unroll=min(5, chunks[c + 1] - chunks[c]))

    for c in range(FIRST):
        finish_chunk(c)

    for d in range(2):
        edge(d).wait_recv()
    for copy in smalls[3:]:
        copy.wait()
    for d in range(2):
        o, e = d, 1 - d
        here = has[d] * coefs[4, o][:1]
        both = here * coefs[4, e][:1]
        sideways = edge_got[d, 8:16, :] * coefs[4, o]
        for i in range(3):
            moved = edge_got[d, i : i + 1, :]
            for gi in range(2):
                g = 2 * d + gi
                moved = moved + (side[g] * roll_up(sideways, WEST[g]))[gi * 3 + i : gi * 3 + i + 1]
            stress[i][o] = stress[i][o] + here * moved
            stress[i][e] = stress[i][e] + both * edge_got[d, 3 + i : 4 + i, :]

    target = lax.broadcasted_iota(jnp.int32, (groups * 8, 128), 0)
    place = lax.broadcasted_iota(jnp.int32, (128, 128), 0)
    summed = jnp.zeros((groups * 8, 128), F32)
    for y in range(2):
        cells = cell[y : y + 1, :]
        high = jnp.where(cells >= 128, 1, 0)
        goal = owner[y : y + 1, :] * 8 + high * 3
        spread = jnp.zeros((groups * 8, 128), F32)
        for i in range(3):
            spread = jnp.where(target == goal + i, stress[i][y], spread)
        table = jnp.where(place == cells - high * 128, 1.0, 0.0).astype(F32)
        summed = summed + lax.dot_general(
            spread,
            table,
            (((1,), (1,)), ((), ())),
            precision=lax.Precision.HIGHEST,
            preferred_element_type=F32,
        )
    parts[...] = summed.reshape(groups, 8, 128)

    @pl.when(my_grp != 0)
    def _():
        pl.semaphore_wait(all_sem, 1)

    for turn in range(1, groups):
        peer = lax.rem(my_grp + turn, groups)
        pltpu.make_async_remote_copy(
            src_ref=parts.at[peer],
            dst_ref=parts_got.at[turn - 1],
            send_sem=part_send_sem,
            recv_sem=part_recv_sem,
            device_id=(peer, my_aa),
            device_id_type=MESH,
        ).start()

    for c in range(FIRST, SECOND):
        finish_chunk(c)

    pltpu.make_async_copy(parts_got, parts_got, part_recv_sem).wait()
    summed = parts[my_grp]
    for turn in range(1, groups):
        summed = summed + parts_got[turn - 1]
    forcing[:, 0:128] = summed[0:3]
    forcing[:, 128:256] = summed[3:6]

    for c in range(SECOND, last):
        finish_chunk(c)

    pltpu.make_async_copy(parts_got, parts_got, part_send_sem).wait()
    for d in range(2):
        tile(d).wait_send()
        edge(d).wait_send()
        whole = got.at[d, :, pl.ds(SKIP[d], 32 - SKIP[d])]
        pltpu.make_async_copy(whole, whole, send_sem.at[d]).wait()


def pass_on(new, forcing, new_out, forcing_out, sem):
    step = -(-new.shape[0] // PIECES)
    pairs = [(forcing, forcing_out)]
    for i in range(PIECES):
        where = pl.ds(i * step, min(step, new.shape[0] - i * step))
        pairs.append((new.at[where], new_out.at[where]))
    stores = [pltpu.make_async_copy(src, dst, sem.at[i]) for i, (src, dst) in enumerate(pairs)]
    for copy in stores:
        copy.start()
    for copy in stores:
        copy.wait()


def on_device(groups, spectrum, friction, wind_dir, wet, owner, cell):
    comps, rows, width = spectrum.shape
    freqs = comps // DIRS
    chunks = CHUNKS if CHUNKS[-1] == freqs else tuple(range(0, freqs + 1, 2))
    last = len(chunks) - 1
    anywhere = pl.BlockSpec(memory_space=pl.ANY)
    dma = pltpu.SemaphoreType.DMA
    results = (
        jax.ShapeDtypeStruct((freqs, 2 * DIRS, width), F32),
        jax.ShapeDtypeStruct((3, 256), F32),
    )
    vmem = pltpu.VMEM
    inside = pl.BlockSpec(memory_space=pltpu.VMEM)
    new, forcing = pl.pallas_call(
        functools.partial(kernel, chunks),
        out_shape=(vmem((freqs, 2 * DIRS, width), F32), vmem((3, 256), F32)),
        in_specs=[anywhere] * 6,
        out_specs=(inside, inside),
        scratch_shapes=[
            vmem((freqs, 2 * DIRS, width), F32),
            vmem((rows, width), F32),
            vmem((rows, width), F32),
            vmem((8, width), jnp.int32),
            vmem((rows, width), jnp.int32),
            vmem((rows, width), jnp.int32),
            vmem((2, freqs, DIRS, width), F32),
            vmem((freqs, 4, 8, width), F32),
            vmem((freqs, 4, 8, width), F32),
            vmem((8, width), F32),
            vmem((2, 8, width), F32),
            vmem((5, 8, 8, width), F32),
            vmem((5, 8, 8, width), F32),
            vmem((2, (freqs + 7) // 8 * 8, width), F32),
            vmem((24, 8, width), F32),
            vmem((2, 16, width), F32),
            vmem((2, 16, width), F32),
            vmem((groups, 8, width), F32),
            vmem((groups - 1, 8, width), F32),
            dma((2,)),
            dma((5,)),
            dma((2,)),
            dma((2, last)),
            dma((2,)),
            dma((2,)),
            dma((2,)),
            dma((2,)),
            dma,
            dma,
            pltpu.SemaphoreType.REGULAR,
            pltpu.SemaphoreType.REGULAR,
        ],
        compiler_params=pltpu.CompilerParams(
            collective_id=0, has_side_effects=True, vmem_limit_bytes=LIMIT
        ),
    )(
        spectrum.reshape(freqs, 2 * DIRS, width),
        friction,
        wind_dir,
        wet,
        owner.reshape(rows, width),
        cell,
    )
    new, forcing = pl.pallas_call(
        pass_on,
        out_shape=results,
        in_specs=[inside] * 2,
        out_specs=(anywhere, anywhere),
        scratch_shapes=[dma((PIECES + 1,))],
        compiler_params=pltpu.CompilerParams(vmem_limit_bytes=4 * 1024 * 1024),
    )(new, forcing)
    return new.reshape(comps, rows, width), forcing


def solution(mesh):
    placed = (
        P(None, ("grp", "aa"), None),
        P(("grp", "aa"), None),
        P(("grp", "aa"), None),
        P("grp", None),
        P(("grp", "aa"), None),
        P(("grp", "aa"), None),
    )
    return jax.shard_map(
        functools.partial(on_device, mesh.shape["grp"]),
        mesh=mesh,
        in_specs=placed,
        out_specs=(P(None, ("grp", "aa"), None), P(None, ("grp", "aa"))),
        check_vma=False,
    )
```

```python
import functools
import math

import jax
import jax.numpy as jnp
from jax import lax
from jax.experimental import pallas as pl
from jax.experimental.pallas import tpu as pltpu
from jax.sharding import PartitionSpec as P

MESH = pl.DeviceIdType.MESH
DIRS = 32
COURANT = 0.7
LOG2E = math.log2(math.e)
CHUNKS = (0, 15, 30, 44, 47, 50)
FIRST, SECOND = 1, 3
PIECES = 4
LIMIT = 60 * 1024 * 1024
F32 = jnp.float32

EDGE = (1, 1, 0, 0)
SKIP = (2, 0)
WEST = (True, False, False, True)


def roll_up(cells, west):
    return pltpu.roll(cells, 1 if west else 127, 1)


def wide(cells):
    return jnp.broadcast_to(cells, (8, 128))


def reduce8(cells):
    return jnp.sum(cells, axis=0, keepdims=True)


def kernel(
    chunks,
    spectrum_hbm,
    friction_hbm,
    wind_hbm,
    wet_hbm,
    owner_hbm,
    cell_hbm,
    stepped,
    forcing,
    spectrum,
    friction,
    wind,
    wet,
    owner,
    cell,
    got,
    passing,
    near,
    far,
    mine,
    others,
    coefs,
    halo,
    scales,
    moments,
    edge_send,
    edge_got,
    parts,
    parts_got,
    load_sem,
    small_sem,
    send_sem,
    recv_sem,
    tile_send_sem,
    tile_recv_sem,
    edge_send_sem,
    edge_recv_sem,
    part_send_sem,
    part_recv_sem,
    pass_send_sem,
    pass_recv_sem,
    row_sem,
    here_sem,
    all_sem,
):
    freqs = spectrum.shape[0]
    groups, column = lax.axis_size("grp"), lax.axis_size("aa")
    my_grp, my_aa = lax.axis_index("grp"), lax.axis_index("aa")
    devices = groups * column
    me = my_grp * column + my_aa
    after = lax.rem(me + 1, devices)
    before = lax.rem(me + devices - 1, devices)
    row_ids = ((after // column, lax.rem(after, column)), (before // column, lax.rem(before, column)))
    last = len(chunks) - 1

    line = 8 if column % 8 == 0 else column
    place_in_line = lax.rem(my_aa, line)
    is_first, is_last = place_in_line == 0, place_in_line == line - 1
    is_inner = jnp.logical_and(place_in_line > 0, place_in_line < line - 1)
    is_early = place_in_line < line - 2
    is_late = place_in_line >= line - 2
    ends = jnp.logical_or(is_first, is_last)

    middle = line // 2
    is_middle, is_low = place_in_line == middle, place_in_line == 1
    ahead = lax.rem(me + line - 1, devices)
    behind = lax.rem(me + devices - (line - 1), devices)
    ahead_id = (ahead // column, lax.rem(ahead, column))
    behind_id = (behind // column, lax.rem(behind, column))
    to_middle, to_low = line - 1 - middle, middle - 1
    barrier = pltpu.get_barrier_semaphore()

    @pl.when(ends)
    def _():
        pl.semaphore_signal(barrier, inc=1, device_id=row_ids[1], device_id_type=MESH)

    @pl.when(is_early)
    def _():
        pl.semaphore_signal(barrier, inc=1, device_id=row_ids[0], device_id_type=MESH)

    @pl.when(is_middle)
    def _():
        pl.semaphore_signal(barrier, inc=1, device_id=(my_grp, my_aa + to_middle), device_id_type=MESH)

    @pl.when(is_low)
    def _():
        pl.semaphore_signal(barrier, inc=1, device_id=(my_grp, my_aa + to_low), device_id_type=MESH)

    @pl.when(is_first)
    def _():
        pl.semaphore_signal(barrier, inc=1, device_id=behind_id, device_id_type=MESH)

    @pl.when(my_grp == 0)
    def _():
        for peer in range(1, groups):
            pl.semaphore_signal(barrier, inc=1, device_id=(peer, my_aa), device_id_type=MESH)

    got[0, :, 0 : SKIP[0], :] = jnp.zeros((freqs, SKIP[0], 128), F32)
    half = freqs // 2
    loads = [
        pltpu.make_async_copy(spectrum_hbm.at[pl.ds(i * half, half)], spectrum.at[pl.ds(i * half, half)], load_sem.at[i])
        for i in range(2)
    ]
    wet_start = pl.multiple_of((2 * my_aa) // 8 * 8, 8)
    smalls = [
        pltpu.make_async_copy(friction_hbm, friction, small_sem.at[0]),
        pltpu.make_async_copy(wind_hbm, wind, small_sem.at[1]),
        pltpu.make_async_copy(wet_hbm.at[pl.ds(wet_start, 8)], wet, small_sem.at[2]),
        pltpu.make_async_copy(owner_hbm, owner, small_sem.at[3]),
        pltpu.make_async_copy(cell_hbm, cell, small_sem.at[4]),
    ]
    rows_heard = jnp.where(is_first, 0, jnp.where(place_in_line == line - 2, 2, 1))
    passes = jnp.logical_or(jnp.logical_or(is_middle, is_low), is_last)
    heard = rows_heard + jnp.where(passes, 1, 0) + jnp.where(my_grp == 0, 0, 1)

    @pl.when(heard > 0)
    def _():
        pl.semaphore_wait(barrier, heard)

    def bulk(d, c):
        where = pl.ds(chunks[c], chunks[c + 1] - chunks[c])
        first = SKIP[d]
        return pltpu.make_async_remote_copy(
            src_ref=spectrum_hbm.at[where, pl.ds(32 * d + first, 32 - first)],
            dst_ref=got.at[d, where, pl.ds(first, 32 - first)],
            send_sem=send_sem.at[d],
            recv_sem=recv_sem.at[d, c],
            device_id=row_ids[d],
            device_id_type=MESH,
        )

    block = pl.ds(chunks[last - 1], chunks[last] - chunks[last - 1])
    lines = pl.ds(SKIP[0], 32 - SKIP[0])

    def hop(source, target, other, sent, landed):
        return pltpu.make_async_remote_copy(
            src_ref=source, dst_ref=target, send_sem=sent, recv_sem=landed, device_id=other, device_id_type=MESH
        )

    passed = passing.at[:, lines]

    @pl.when(is_late)
    def _():
        bulk(0, 0).start()

    @pl.when(is_last)
    def _():
        hop(
            spectrum_hbm.at[block, lines],
            passed,
            (my_grp, my_aa - to_middle),
            send_sem.at[0],
            pass_recv_sem,
        ).start()

    @pl.when(is_inner)
    def _():
        bulk(1, 0).start()
        pl.semaphore_signal(row_sem.at[0], inc=1, device_id=row_ids[1], device_id_type=MESH)

    @pl.when(is_late)
    def _():
        pl.semaphore_signal(row_sem.at[1], inc=1, device_id=row_ids[0], device_id_type=MESH)

    for copy in smalls[:3] + loads + smalls[3:]:
        copy.start()

    @pl.when(is_early)
    def _():
        pl.semaphore_wait(row_sem.at[0], 1)
        bulk(0, 0).start()

    @pl.when(my_grp != 0)
    def _():
        pl.semaphore_signal(here_sem, inc=1, device_id=(0, my_aa), device_id_type=MESH)

    lane = lax.broadcasted_iota(jnp.int32, (8, 128), 1)
    place8 = lax.broadcasted_iota(jnp.int32, (8, 128), 0)
    cos0 = jnp.full((8, 128), 1.0, F32)
    sin0 = jnp.full((8, 128), 0.0, F32)
    for j in range(1, 8):
        cos0 = jnp.where(place8 == j, F32(math.cos(2.0 * math.pi * j / DIRS)), cos0)
        sin0 = jnp.where(place8 == j, F32(math.sin(2.0 * math.pi * j / DIRS)), sin0)
    cosine = (cos0, -sin0, -cos0, sin0)
    sine = (sin0, cos0, -sin0, -cos0)
    abs_x = [COURANT * c for c in (cos0, sin0, cos0, sin0)]
    abs_y = [COURANT * c for c in (sin0, cos0, sin0, cos0)]
    speed_sum = COURANT * (cos0 + sin0)
    side = [jnp.where(lane != 0, 1.0, 0.0) if west else jnp.where(lane != 127, 1.0, 0.0) for west in WEST]
    number = lax.broadcasted_iota(jnp.int32, scales.shape[1:], 0).astype(F32) * F32(1.0 / max(freqs - 1, 1))
    scales[0] = number
    scales[1] = jnp.exp2(-number)
    edge_send[...] = jnp.zeros_like(edge_send)
    has = [jnp.where(me > 0, 1.0, 0.0).astype(F32), jnp.where(me < devices - 1, 1.0, 0.0).astype(F32)]

    for copy in smalls[:3]:
        copy.wait()
    grow = 0.4 * friction[...]
    mine[0:2, :] = grow * jnp.cos(wind[...])
    mine[2:4, :] = grow * jnp.sin(wind[...])
    wet_row = lax.rem(2 * my_aa, 8)
    for y in range(2):
        mine[6 + y : 7 + y, :] = wet[pl.ds(wet_row + y, 1), :].astype(F32)

    def add(k, acc):
        return acc + jnp.sum(spectrum[k].reshape(8, 8, 128), axis=0)

    acc = jnp.zeros((8, 128), F32)
    for i in range(2):
        loads[i].wait()
        acc = lax.fori_loop(i * half, (i + 1) * half, add, acc)
    for y in range(2):
        total = reduce8(jnp.where(lax.rem(place8, 2) == y, acc, 0.0)) / F32(freqs * DIRS)
        mine[4 + y : 5 + y, :] = total / (1.0 + total)

    def tile(d):
        return pltpu.make_async_remote_copy(
            src_ref=mine,
            dst_ref=others.at[d],
            send_sem=tile_send_sem.at[d],
            recv_sem=tile_recv_sem.at[d],
            device_id=row_ids[d],
            device_id_type=MESH,
        )

    tile(0).start()

    @pl.when(is_inner)
    def _():
        tile(1).start()

    def exponent(values, g, y):
        growth = jnp.maximum(cosine[g] * values[0 + y : 1 + y] + sine[g] * values[2 + y : 3 + y], 0.0)
        damp = values[4 + y : 5 + y]
        return LOG2E * (0.5 * growth - 0.15 * damp), LOG2E * (growth - 0.6 * damp)

    values = mine[...]
    for g in range(4):
        for y in range(2):
            coefs[0, g * 2 + y], coefs[1, g * 2 + y] = exponent(values, g, y)
            coefs[2, g * 2 + y] = values[6 + y : 7 + y] * side[g] * abs_x[g]
            pull = values[6 + y : 7 + y] * abs_y[g]
            coefs[3, g * 2 + y] = pull if y == EDGE[g] else pull * has[g // 2]
    for y in range(2):
        coefs[4, y] = wide(values[6 + y : 7 + y])
    coefs[4, 2] = speed_sum

    def scale(index, k):
        return wide(scales[index, pl.ds(k, 1), :])

    def slope(g, y, cells, other):
        pulled = coefs[2, g * 2 + y] * roll_up(cells, WEST[g])
        if other is not None:
            pulled = pulled + coefs[3, g * 2 + y] * other
        return coefs[4, 2] * cells - pulled

    for d in range(2):

        def make(k, sums, d=d):
            q, s = scale(0, k), scale(1, k)
            new = []
            for gi in range(2):
                g = 2 * d + gi
                e = EDGE[g]
                energy = []
                for y in range(2):
                    cells = spectrum[k, pl.ds(g * 16 + y, 8, stride=2), :]
                    power = jnp.exp2(coefs[0, g * 2 + y] + q * coefs[1, g * 2 + y])
                    energy.append(coefs[4, y] * cells * power)
                    first = s * energy[y]
                    old = sums[(gi * 2 + y) * 3 : (gi * 2 + y) * 3 + 3]
                    new += [old[0] + energy[y], old[1] + first, old[2] + s * first]
                near[k, g] = energy[1 - e]
                far[k, g] = energy[e] - s * slope(g, e, energy[e], energy[1 - e])
            return tuple(new)

        sums = lax.fori_loop(0, freqs, make, (jnp.zeros((8, 128), F32),) * 12, unroll=10)
        for i in range(12):
            moments[d * 12 + i] = sums[i]

    def weigh(g):
        per = F32(1.0 / (freqs * DIRS))
        return (
            0.5 * per * cosine[g] * cosine[g],
            0.5 * per * cosine[g] * sine[g],
            0.5 * per * sine[g] * sine[g],
        )

    own = [[jnp.zeros((8, 128), F32) for _ in range(2)] for _ in range(3)]
    for d in range(2):
        direct = [jnp.zeros((8, 128), F32) for _ in range(3)]
        double = [jnp.zeros((8, 128), F32) for _ in range(3)]
        for gi in range(2):
            g = 2 * d + gi
            e = EDGE[g]
            o = 1 - e
            m_e = [moments[g * 6 + e * 3 + m] for m in range(3)]
            m_o = [moments[g * 6 + o * 3 + m] for m in range(3)]
            slope_o2 = slope(g, o, m_o[2], None)
            slope_e2 = slope(g, e, m_e[2], m_o[2])
            sum_o = m_o[0] - 2.0 * slope(g, o, m_o[1], None) + slope(g, o, slope_o2, None)
            sum_e = m_e[0] - 2.0 * slope(g, e, m_e[1], m_o[1]) + slope(g, e, slope_e2, slope_o2)
            weights = weigh(g)
            reach = abs_y[g] * (2.0 * m_e[1] - speed_sum * m_e[2] - slope_e2)
            sideways = abs_x[g] * abs_y[g] * m_e[2]
            twice = abs_y[g] * abs_y[g] * m_e[2]
            for i in range(3):
                own[i][e] = own[i][e] + weights[i] * sum_e
                own[i][o] = own[i][o] + weights[i] * sum_o
                direct[i] = direct[i] + weights[i] * reach
                double[i] = double[i] + weights[i] * twice
                edge_send[d, 8 + gi * 3 + i : 9 + gi * 3 + i, :] = reduce8(weights[i] * sideways)
        for i in range(3):
            edge_send[d, i : i + 1, :] = reduce8(direct[i])
            edge_send[d, 3 + i : 4 + i, :] = reduce8(double[i])

    def edge(d):
        return pltpu.make_async_remote_copy(
            src_ref=edge_send.at[d],
            dst_ref=edge_got.at[d],
            send_sem=edge_send_sem.at[d],
            recv_sem=edge_recv_sem.at[d],
            device_id=row_ids[d],
            device_id_type=MESH,
        )

    edge(0).start()
    for c in range(1, last - 1):
        bulk(0, c).start()

    @pl.when(jnp.logical_not(is_last))
    def _():
        bulk(0, last - 1).start()

    @pl.when(is_inner)
    def _():
        edge(1).start()

    @pl.when(jnp.logical_and(is_inner, jnp.logical_not(is_middle)))
    def _():
        for c in range(1, last):
            bulk(1, c).start()

    @pl.when(ends)
    def _():
        pl.semaphore_wait(row_sem.at[1], 1)
        tile(1).start()
        edge(1).start()
        for c in range(last):
            bulk(1, c).start()

    @pl.when(my_grp == 0)
    def _():
        pl.semaphore_wait(here_sem, groups - 1)
        for peer in range(1, groups):
            pl.semaphore_signal(all_sem, inc=1, device_id=(peer, my_aa), device_id_type=MESH)

    stress = [[reduce8(own[i][y]) for y in range(2)] for i in range(3)]

    for d in range(2):
        tile(d).wait_recv()
        values = others[d]
        for g in (2 * d, 2 * d + 1):
            e = EDGE[g]
            for y in range(2):
                halo[0, g * 2 + y], halo[1, g * 2 + y] = exponent(values, g, y)
            halo[2, g] = values[6 + e : 7 + e] * side[g] * abs_x[g]
            halo[3, g] = values[6 + e : 7 + e] * abs_y[g]
        for y in range(2):
            halo[4, d * 2 + y] = wide(values[6 + y : 7 + y])

    def finish(k, carry):
        q, s = scale(0, k), scale(1, k)
        for g in range(4):
            d, e = g // 2, EDGE[g]
            o = 1 - e
            base = (g % 2) * 16
            there = []
            for y in range(2):
                cells = got[d, k, pl.ds(base + y, 8, stride=2), :]
                power = jnp.exp2(halo[0, g * 2 + y] + q * halo[1, g * 2 + y])
                there.append(halo[4, d * 2 + y] * cells * power)
            pulled = halo[2, g] * roll_up(there[e], WEST[g]) + halo[3, g] * there[o]
            there_one = there[e] - s * (coefs[4, 2] * there[e] - pulled)
            start_o = near[k, g]
            one_e = far[k, g]
            one_o = start_o - s * slope(g, o, start_o, there[e])
            two_o = one_o - s * slope(g, o, one_o, there_one)
            two_e = one_e - s * slope(g, e, one_e, one_o)
            stepped[k, pl.ds(g * 16 + o, 8, stride=2), :] = two_o
            stepped[k, pl.ds(g * 16 + e, 8, stride=2), :] = two_e
        return carry

    def finish_chunk(c):
        for d in range(2):
            bulk(d, c).wait_recv()
        lax.fori_loop(chunks[c], chunks[c + 1], finish, 0, unroll=min(5, chunks[c + 1] - chunks[c]))

    for c in range(FIRST):
        finish_chunk(c)

    onward = hop(passed, passed, (my_grp, my_aa - to_low), pass_send_sem, pass_recv_sem)
    home = hop(passed, got.at[0, block, lines], ahead_id, pass_send_sem, recv_sem.at[0, last - 1])
    arrived = pltpu.make_async_copy(passed, passed, pass_recv_sem)

    @pl.when(is_middle)
    def _():
        arrived.wait()
        onward.start()
        for c in range(1, last):
            bulk(1, c).start()

    for d in range(2):
        edge(d).wait_recv()
    for copy in smalls[3:]:
        copy.wait()
    for d in range(2):
        o, e = d, 1 - d
        here = has[d] * coefs[4, o][:1]
        both = here * coefs[4, e][:1]
        sideways = edge_got[d, 8:16, :] * coefs[4, o]
        for i in range(3):
            moved = edge_got[d, i : i + 1, :]
            for gi in range(2):
                g = 2 * d + gi
                moved = moved + (side[g] * roll_up(sideways, WEST[g]))[gi * 3 + i : gi * 3 + i + 1]
            stress[i][o] = stress[i][o] + here * moved
            stress[i][e] = stress[i][e] + both * edge_got[d, 3 + i : 4 + i, :]

    target = lax.broadcasted_iota(jnp.int32, (groups * 8, 128), 0)
    place = lax.broadcasted_iota(jnp.int32, (128, 128), 0)
    summed = jnp.zeros((groups * 8, 128), F32)
    for y in range(2):
        cells = cell[y : y + 1, :]
        high = jnp.where(cells >= 128, 1, 0)
        goal = owner[y : y + 1, :] * 8 + high * 3
        spread = jnp.zeros((groups * 8, 128), F32)
        for i in range(3):
            spread = jnp.where(target == goal + i, stress[i][y], spread)
        table = jnp.where(place == cells - high * 128, 1.0, 0.0).astype(F32)
        summed = summed + lax.dot_general(
            spread,
            table,
            (((1,), (1,)), ((), ())),
            precision=lax.Precision.HIGHEST,
            preferred_element_type=F32,
        )
    parts[...] = summed.reshape(groups, 8, 128)

    @pl.when(my_grp != 0)
    def _():
        pl.semaphore_wait(all_sem, 1)

    for turn in range(1, groups):
        peer = lax.rem(my_grp + turn, groups)
        pltpu.make_async_remote_copy(
            src_ref=parts.at[peer],
            dst_ref=parts_got.at[turn - 1],
            send_sem=part_send_sem,
            recv_sem=part_recv_sem,
            device_id=(peer, my_aa),
            device_id_type=MESH,
        ).start()

    for c in range(FIRST, SECOND):
        finish_chunk(c)

    pltpu.make_async_copy(parts_got, parts_got, part_recv_sem).wait()
    summed = parts[my_grp]
    for turn in range(1, groups):
        summed = summed + parts_got[turn - 1]
    forcing[:, 0:128] = summed[0:3]
    forcing[:, 128:256] = summed[3:6]

    for c in range(SECOND, last):
        finish_chunk(c)

    @pl.when(is_low)
    def _():
        arrived.wait()
        home.start()
        home.wait_send()

    @pl.when(is_middle)
    def _():
        onward.wait_send()

    pltpu.make_async_copy(parts_got, parts_got, part_send_sem).wait()
    for d in range(2):
        tile(d).wait_send()
        edge(d).wait_send()
        whole = got.at[d, :, pl.ds(SKIP[d], 32 - SKIP[d])]
        pltpu.make_async_copy(whole, whole, send_sem.at[d]).wait()


def pass_on(new, forcing, new_out, forcing_out, sem):
    step = -(-new.shape[0] // PIECES)
    pairs = [(forcing, forcing_out)]
    for i in range(PIECES):
        where = pl.ds(i * step, min(step, new.shape[0] - i * step))
        pairs.append((new.at[where], new_out.at[where]))
    stores = [pltpu.make_async_copy(src, dst, sem.at[i]) for i, (src, dst) in enumerate(pairs)]
    for copy in stores:
        copy.start()
    for copy in stores:
        copy.wait()


def on_device(groups, spectrum, friction, wind_dir, wet, owner, cell):
    comps, rows, width = spectrum.shape
    freqs = comps // DIRS
    chunks = CHUNKS if CHUNKS[-1] == freqs else tuple(range(0, freqs + 1, 2))
    last = len(chunks) - 1
    anywhere = pl.BlockSpec(memory_space=pl.ANY)
    dma = pltpu.SemaphoreType.DMA
    results = (
        jax.ShapeDtypeStruct((freqs, 2 * DIRS, width), F32),
        jax.ShapeDtypeStruct((3, 256), F32),
    )
    vmem = pltpu.VMEM
    inside = pl.BlockSpec(memory_space=pltpu.VMEM)
    new, forcing = pl.pallas_call(
        functools.partial(kernel, chunks),
        out_shape=(vmem((freqs, 2 * DIRS, width), F32), vmem((3, 256), F32)),
        in_specs=[anywhere] * 6,
        out_specs=(inside, inside),
        scratch_shapes=[
            vmem((freqs, 2 * DIRS, width), F32),
            vmem((rows, width), F32),
            vmem((rows, width), F32),
            vmem((8, width), jnp.int32),
            vmem((rows, width), jnp.int32),
            vmem((rows, width), jnp.int32),
            vmem((2, freqs, DIRS, width), F32),
            vmem((chunks[last] - chunks[last - 1], DIRS, width), F32),
            vmem((freqs, 4, 8, width), F32),
            vmem((freqs, 4, 8, width), F32),
            vmem((8, width), F32),
            vmem((2, 8, width), F32),
            vmem((5, 8, 8, width), F32),
            vmem((5, 8, 8, width), F32),
            vmem((2, (freqs + 7) // 8 * 8, width), F32),
            vmem((24, 8, width), F32),
            vmem((2, 16, width), F32),
            vmem((2, 16, width), F32),
            vmem((groups, 8, width), F32),
            vmem((groups - 1, 8, width), F32),
            dma((2,)),
            dma((5,)),
            dma((2,)),
            dma((2, last)),
            dma((2,)),
            dma((2,)),
            dma((2,)),
            dma((2,)),
            dma,
            dma,
            dma,
            dma,
            pltpu.SemaphoreType.REGULAR((2,)),
            pltpu.SemaphoreType.REGULAR,
            pltpu.SemaphoreType.REGULAR,
        ],
        compiler_params=pltpu.CompilerParams(
            collective_id=0, has_side_effects=True, vmem_limit_bytes=LIMIT
        ),
    )(
        spectrum.reshape(freqs, 2 * DIRS, width),
        friction,
        wind_dir,
        wet,
        owner.reshape(rows, width),
        cell,
    )
    new, forcing = pl.pallas_call(
        pass_on,
        out_shape=results,
        in_specs=[inside] * 2,
        out_specs=(anywhere, anywhere),
        scratch_shapes=[dma((PIECES + 1,))],
        compiler_params=pltpu.CompilerParams(vmem_limit_bytes=4 * 1024 * 1024),
    )(new, forcing)
    return new.reshape(comps, rows, width), forcing


def solution(mesh):
    placed = (
        P(None, ("grp", "aa"), None),
        P(("grp", "aa"), None),
        P(("grp", "aa"), None),
        P("grp", None),
        P(("grp", "aa"), None),
        P(("grp", "aa"), None),
    )
    return jax.shard_map(
        functools.partial(on_device, mesh.shape["grp"]),
        mesh=mesh,
        in_specs=placed,
        out_specs=(P(None, ("grp", "aa"), None), P(None, ("grp", "aa"))),
        check_vma=False,
    )
```

```python
import functools
import math

import jax
import jax.numpy as jnp
from jax import lax
from jax.experimental import pallas as pl
from jax.experimental.pallas import tpu as pltpu
from jax.sharding import PartitionSpec as P

MESH = pl.DeviceIdType.MESH
DIRS = 32
COURANT = 0.7
LOG2E = math.log2(math.e)
CHUNKS = (0, 10, 28, 44, 47, 50)
FIRST, SECOND = 1, 4
PIECES = 4
LIMIT = 60 * 1024 * 1024
F32 = jnp.float32

EDGE = (1, 1, 0, 0)
SKIP = (2, 0)
WEST = (True, False, False, True)


def roll_up(cells, west):
    return pltpu.roll(cells, 1 if west else 127, 1)


def wide(cells):
    return jnp.broadcast_to(cells, (8, 128))


def reduce8(cells):
    return jnp.sum(cells, axis=0, keepdims=True)


def kernel(
    chunks,
    spectrum_hbm,
    friction_hbm,
    wind_hbm,
    wet_hbm,
    owner_hbm,
    cell_hbm,
    stepped,
    forcing,
    spectrum,
    friction,
    wind,
    wet,
    owner,
    cell,
    got,
    passing,
    near,
    far,
    mine,
    others,
    coefs,
    halo,
    scales,
    moments,
    edge_send,
    edge_got,
    parts,
    parts_got,
    load_sem,
    small_sem,
    send_sem,
    recv_sem,
    tile_send_sem,
    tile_recv_sem,
    edge_send_sem,
    edge_recv_sem,
    part_send_sem,
    part_recv_sem,
    pass_send_sem,
    pass_recv_sem,
    row_sem,
    here_sem,
    all_sem,
):
    freqs = spectrum.shape[0]
    groups, column = lax.axis_size("grp"), lax.axis_size("aa")
    my_grp, my_aa = lax.axis_index("grp"), lax.axis_index("aa")
    devices = groups * column
    me = my_grp * column + my_aa
    after = lax.rem(me + 1, devices)
    before = lax.rem(me + devices - 1, devices)
    row_ids = ((after // column, lax.rem(after, column)), (before // column, lax.rem(before, column)))
    last = len(chunks) - 1

    line = 8 if column % 8 == 0 else column
    place_in_line = lax.rem(my_aa, line)
    is_first, is_last = place_in_line == 0, place_in_line == line - 1
    is_inner = jnp.logical_and(place_in_line > 0, place_in_line < line - 1)
    is_early = place_in_line < line - 2
    is_late = place_in_line >= line - 2
    ends = jnp.logical_or(is_first, is_last)

    middle = line // 2
    is_middle, is_low = place_in_line == middle, place_in_line == 1
    ahead = lax.rem(me + line - 1, devices)
    behind = lax.rem(me + devices - (line - 1), devices)
    ahead_id = (ahead // column, lax.rem(ahead, column))
    behind_id = (behind // column, lax.rem(behind, column))
    to_middle, to_low = line - 1 - middle, middle - 1
    barrier = pltpu.get_barrier_semaphore()

    @pl.when(ends)
    def _():
        pl.semaphore_signal(barrier, inc=1, device_id=row_ids[1], device_id_type=MESH)

    @pl.when(is_early)
    def _():
        pl.semaphore_signal(barrier, inc=1, device_id=row_ids[0], device_id_type=MESH)

    @pl.when(is_middle)
    def _():
        pl.semaphore_signal(barrier, inc=1, device_id=(my_grp, my_aa + to_middle), device_id_type=MESH)

    @pl.when(is_low)
    def _():
        pl.semaphore_signal(barrier, inc=1, device_id=(my_grp, my_aa + to_low), device_id_type=MESH)

    @pl.when(is_first)
    def _():
        pl.semaphore_signal(barrier, inc=1, device_id=behind_id, device_id_type=MESH)

    @pl.when(my_grp == 0)
    def _():
        for peer in range(1, groups):
            pl.semaphore_signal(barrier, inc=1, device_id=(peer, my_aa), device_id_type=MESH)

    got[0, :, 0 : SKIP[0], :] = jnp.zeros((freqs, SKIP[0], 128), F32)
    half = freqs // 2
    loads = [
        pltpu.make_async_copy(spectrum_hbm.at[pl.ds(i * half, half)], spectrum.at[pl.ds(i * half, half)], load_sem.at[i])
        for i in range(2)
    ]
    wet_start = pl.multiple_of((2 * my_aa) // 8 * 8, 8)
    smalls = [
        pltpu.make_async_copy(friction_hbm, friction, small_sem.at[0]),
        pltpu.make_async_copy(wind_hbm, wind, small_sem.at[1]),
        pltpu.make_async_copy(wet_hbm.at[pl.ds(wet_start, 8)], wet, small_sem.at[2]),
        pltpu.make_async_copy(owner_hbm, owner, small_sem.at[3]),
        pltpu.make_async_copy(cell_hbm, cell, small_sem.at[4]),
    ]
    rows_heard = jnp.where(is_first, 0, jnp.where(place_in_line == line - 2, 2, 1))
    passes = jnp.logical_or(jnp.logical_or(is_middle, is_low), is_last)
    heard = rows_heard + jnp.where(passes, 1, 0) + jnp.where(my_grp == 0, 0, 1)

    @pl.when(heard > 0)
    def _():
        pl.semaphore_wait(barrier, heard)

    def bulk(d, c):
        where = pl.ds(chunks[c], chunks[c + 1] - chunks[c])
        first = SKIP[d]
        return pltpu.make_async_remote_copy(
            src_ref=spectrum_hbm.at[where, pl.ds(32 * d + first, 32 - first)],
            dst_ref=got.at[d, where, pl.ds(first, 32 - first)],
            send_sem=send_sem.at[d],
            recv_sem=recv_sem.at[d, c],
            device_id=row_ids[d],
            device_id_type=MESH,
        )

    block = pl.ds(chunks[last - 1], chunks[last] - chunks[last - 1])
    lines = pl.ds(SKIP[0], 32 - SKIP[0])

    def hop(source, target, other, sent, landed):
        return pltpu.make_async_remote_copy(
            src_ref=source, dst_ref=target, send_sem=sent, recv_sem=landed, device_id=other, device_id_type=MESH
        )

    passed = passing.at[:, lines]

    @pl.when(is_late)
    def _():
        pl.semaphore_signal(row_sem.at[1], inc=1, device_id=row_ids[0], device_id_type=MESH)
        bulk(0, 0).start()

    @pl.when(is_last)
    def _():
        hop(
            spectrum_hbm.at[block, lines],
            passed,
            (my_grp, my_aa - to_middle),
            send_sem.at[0],
            pass_recv_sem,
        ).start()

    @pl.when(is_inner)
    def _():
        bulk(1, 0).start()
        pl.semaphore_signal(row_sem.at[0], inc=1, device_id=row_ids[1], device_id_type=MESH)

    for copy in smalls[:3] + loads + smalls[3:]:
        copy.start()

    @pl.when(is_early)
    def _():
        pl.semaphore_wait(row_sem.at[0], 1)
        bulk(0, 0).start()

    @pl.when(my_grp != 0)
    def _():
        pl.semaphore_signal(here_sem, inc=1, device_id=(0, my_aa), device_id_type=MESH)

    lane = lax.broadcasted_iota(jnp.int32, (8, 128), 1)
    place8 = lax.broadcasted_iota(jnp.int32, (8, 128), 0)
    cos0 = jnp.full((8, 128), 1.0, F32)
    sin0 = jnp.full((8, 128), 0.0, F32)
    for j in range(1, 8):
        cos0 = jnp.where(place8 == j, F32(math.cos(2.0 * math.pi * j / DIRS)), cos0)
        sin0 = jnp.where(place8 == j, F32(math.sin(2.0 * math.pi * j / DIRS)), sin0)
    cosine = (cos0, -sin0, -cos0, sin0)
    sine = (sin0, cos0, -sin0, -cos0)
    abs_x = [COURANT * c for c in (cos0, sin0, cos0, sin0)]
    abs_y = [COURANT * c for c in (sin0, cos0, sin0, cos0)]
    speed_sum = COURANT * (cos0 + sin0)
    side = [jnp.where(lane != 0, 1.0, 0.0) if west else jnp.where(lane != 127, 1.0, 0.0) for west in WEST]
    number = lax.broadcasted_iota(jnp.int32, scales.shape[1:], 0).astype(F32) * F32(1.0 / max(freqs - 1, 1))
    scales[0] = number
    scales[1] = jnp.exp2(-number)
    edge_send[...] = jnp.zeros_like(edge_send)
    has = [jnp.where(me > 0, 1.0, 0.0).astype(F32), jnp.where(me < devices - 1, 1.0, 0.0).astype(F32)]

    for copy in smalls[:3]:
        copy.wait()
    grow = 0.4 * friction[...]
    mine[0:2, :] = grow * jnp.cos(wind[...])
    mine[2:4, :] = grow * jnp.sin(wind[...])
    wet_row = lax.rem(2 * my_aa, 8)
    for y in range(2):
        mine[6 + y : 7 + y, :] = wet[pl.ds(wet_row + y, 1), :].astype(F32)

    def add(k, acc):
        return acc + jnp.sum(spectrum[k].reshape(8, 8, 128), axis=0)

    acc = jnp.zeros((8, 128), F32)
    for i in range(2):
        loads[i].wait()
        acc = lax.fori_loop(i * half, (i + 1) * half, add, acc)
    for y in range(2):
        total = reduce8(jnp.where(lax.rem(place8, 2) == y, acc, 0.0)) / F32(freqs * DIRS)
        mine[4 + y : 5 + y, :] = total / (1.0 + total)

    def tile(d):
        return pltpu.make_async_remote_copy(
            src_ref=mine,
            dst_ref=others.at[d],
            send_sem=tile_send_sem.at[d],
            recv_sem=tile_recv_sem.at[d],
            device_id=row_ids[d],
            device_id_type=MESH,
        )

    tile(0).start()

    @pl.when(is_inner)
    def _():
        tile(1).start()

    def exponent(values, g, y):
        growth = jnp.maximum(cosine[g] * values[0 + y : 1 + y] + sine[g] * values[2 + y : 3 + y], 0.0)
        damp = values[4 + y : 5 + y]
        return LOG2E * (0.5 * growth - 0.15 * damp), LOG2E * (growth - 0.6 * damp)

    values = mine[...]
    for g in range(4):
        for y in range(2):
            coefs[0, g * 2 + y], coefs[1, g * 2 + y] = exponent(values, g, y)
            coefs[2, g * 2 + y] = values[6 + y : 7 + y] * side[g] * abs_x[g]
            pull = values[6 + y : 7 + y] * abs_y[g]
            coefs[3, g * 2 + y] = pull if y == EDGE[g] else pull * has[g // 2]
    for y in range(2):
        coefs[4, y] = wide(values[6 + y : 7 + y])
    coefs[4, 2] = speed_sum

    def scale(index, k):
        return wide(scales[index, pl.ds(k, 1), :])

    def slope(g, y, cells, other):
        pulled = coefs[2, g * 2 + y] * roll_up(cells, WEST[g])
        if other is not None:
            pulled = pulled + coefs[3, g * 2 + y] * other
        return coefs[4, 2] * cells - pulled

    for d in range(2):

        def make(k, sums, d=d):
            q, s = scale(0, k), scale(1, k)
            new = []
            for gi in range(2):
                g = 2 * d + gi
                e = EDGE[g]
                energy = []
                for y in range(2):
                    cells = spectrum[k, pl.ds(g * 16 + y, 8, stride=2), :]
                    power = jnp.exp2(coefs[0, g * 2 + y] + q * coefs[1, g * 2 + y])
                    energy.append(coefs[4, y] * cells * power)
                    first = s * energy[y]
                    old = sums[(gi * 2 + y) * 3 : (gi * 2 + y) * 3 + 3]
                    new += [old[0] + energy[y], old[1] + first, old[2] + s * first]
                near[k, g] = energy[1 - e]
                far[k, g] = energy[e] - s * slope(g, e, energy[e], energy[1 - e])
            return tuple(new)

        sums = lax.fori_loop(0, freqs, make, (jnp.zeros((8, 128), F32),) * 12, unroll=10)
        for i in range(12):
            moments[d * 12 + i] = sums[i]

    def weigh(g):
        per = F32(1.0 / (freqs * DIRS))
        return (
            0.5 * per * cosine[g] * cosine[g],
            0.5 * per * cosine[g] * sine[g],
            0.5 * per * sine[g] * sine[g],
        )

    own = [[jnp.zeros((8, 128), F32) for _ in range(2)] for _ in range(3)]
    for d in range(2):
        direct = [jnp.zeros((8, 128), F32) for _ in range(3)]
        double = [jnp.zeros((8, 128), F32) for _ in range(3)]
        for gi in range(2):
            g = 2 * d + gi
            e = EDGE[g]
            o = 1 - e
            m_e = [moments[g * 6 + e * 3 + m] for m in range(3)]
            m_o = [moments[g * 6 + o * 3 + m] for m in range(3)]
            slope_o2 = slope(g, o, m_o[2], None)
            slope_e2 = slope(g, e, m_e[2], m_o[2])
            sum_o = m_o[0] - 2.0 * slope(g, o, m_o[1], None) + slope(g, o, slope_o2, None)
            sum_e = m_e[0] - 2.0 * slope(g, e, m_e[1], m_o[1]) + slope(g, e, slope_e2, slope_o2)
            weights = weigh(g)
            reach = abs_y[g] * (2.0 * m_e[1] - speed_sum * m_e[2] - slope_e2)
            sideways = abs_x[g] * abs_y[g] * m_e[2]
            twice = abs_y[g] * abs_y[g] * m_e[2]
            for i in range(3):
                own[i][e] = own[i][e] + weights[i] * sum_e
                own[i][o] = own[i][o] + weights[i] * sum_o
                direct[i] = direct[i] + weights[i] * reach
                double[i] = double[i] + weights[i] * twice
                edge_send[d, 8 + gi * 3 + i : 9 + gi * 3 + i, :] = reduce8(weights[i] * sideways)
        for i in range(3):
            edge_send[d, i : i + 1, :] = reduce8(direct[i])
            edge_send[d, 3 + i : 4 + i, :] = reduce8(double[i])

    def edge(d):
        return pltpu.make_async_remote_copy(
            src_ref=edge_send.at[d],
            dst_ref=edge_got.at[d],
            send_sem=edge_send_sem.at[d],
            recv_sem=edge_recv_sem.at[d],
            device_id=row_ids[d],
            device_id_type=MESH,
        )

    edge(0).start()
    for c in range(1, last - 1):
        bulk(0, c).start()

    @pl.when(jnp.logical_not(is_last))
    def _():
        bulk(0, last - 1).start()

    @pl.when(is_inner)
    def _():
        edge(1).start()

    @pl.when(jnp.logical_and(is_inner, jnp.logical_not(is_middle)))
    def _():
        for c in range(1, last):
            bulk(1, c).start()

    @pl.when(ends)
    def _():
        pl.semaphore_wait(row_sem.at[1], 1)
        tile(1).start()
        edge(1).start()
        for c in range(last):
            bulk(1, c).start()

    @pl.when(my_grp == 0)
    def _():
        pl.semaphore_wait(here_sem, groups - 1)
        for peer in range(1, groups):
            pl.semaphore_signal(all_sem, inc=1, device_id=(peer, my_aa), device_id_type=MESH)

    stress = [[reduce8(own[i][y]) for y in range(2)] for i in range(3)]

    for d in range(2):
        tile(d).wait_recv()
        values = others[d]
        for g in (2 * d, 2 * d + 1):
            e = EDGE[g]
            for y in range(2):
                halo[0, g * 2 + y], halo[1, g * 2 + y] = exponent(values, g, y)
            halo[2, g] = values[6 + e : 7 + e] * side[g] * abs_x[g]
            halo[3, g] = values[6 + e : 7 + e] * abs_y[g]
        for y in range(2):
            halo[4, d * 2 + y] = wide(values[6 + y : 7 + y])

    def finish(k, carry):
        q, s = scale(0, k), scale(1, k)
        for g in range(4):
            d, e = g // 2, EDGE[g]
            o = 1 - e
            base = (g % 2) * 16
            there = []
            for y in range(2):
                cells = got[d, k, pl.ds(base + y, 8, stride=2), :]
                power = jnp.exp2(halo[0, g * 2 + y] + q * halo[1, g * 2 + y])
                there.append(halo[4, d * 2 + y] * cells * power)
            pulled = halo[2, g] * roll_up(there[e], WEST[g]) + halo[3, g] * there[o]
            there_one = there[e] - s * (coefs[4, 2] * there[e] - pulled)
            start_o = near[k, g]
            one_e = far[k, g]
            one_o = start_o - s * slope(g, o, start_o, there[e])
            two_o = one_o - s * slope(g, o, one_o, there_one)
            two_e = one_e - s * slope(g, e, one_e, one_o)
            stepped[k, pl.ds(g * 16 + o, 8, stride=2), :] = two_o
            stepped[k, pl.ds(g * 16 + e, 8, stride=2), :] = two_e
        return carry

    def finish_chunk(c):
        for d in range(2):
            bulk(d, c).wait_recv()
        lax.fori_loop(chunks[c], chunks[c + 1], finish, 0, unroll=min(5, chunks[c + 1] - chunks[c]))

    for c in range(FIRST):
        finish_chunk(c)

    onward = hop(passed, passed, (my_grp, my_aa - to_low), pass_send_sem, pass_recv_sem)
    home = hop(passed, got.at[0, block, lines], ahead_id, pass_send_sem, recv_sem.at[0, last - 1])
    arrived = pltpu.make_async_copy(passed, passed, pass_recv_sem)

    @pl.when(is_middle)
    def _():
        arrived.wait()
        onward.start()
        for c in range(1, last):
            bulk(1, c).start()

    for d in range(2):
        edge(d).wait_recv()
    for copy in smalls[3:]:
        copy.wait()
    for d in range(2):
        o, e = d, 1 - d
        here = has[d] * coefs[4, o][:1]
        both = here * coefs[4, e][:1]
        sideways = edge_got[d, 8:16, :] * coefs[4, o]
        for i in range(3):
            moved = edge_got[d, i : i + 1, :]
            for gi in range(2):
                g = 2 * d + gi
                moved = moved + (side[g] * roll_up(sideways, WEST[g]))[gi * 3 + i : gi * 3 + i + 1]
            stress[i][o] = stress[i][o] + here * moved
            stress[i][e] = stress[i][e] + both * edge_got[d, 3 + i : 4 + i, :]

    target = lax.broadcasted_iota(jnp.int32, (groups * 8, 128), 0)
    place = lax.broadcasted_iota(jnp.int32, (128, 128), 0)
    summed = jnp.zeros((groups * 8, 128), F32)
    for y in range(2):
        cells = cell[y : y + 1, :]
        high = jnp.where(cells >= 128, 1, 0)
        goal = owner[y : y + 1, :] * 8 + high * 3
        spread = jnp.zeros((groups * 8, 128), F32)
        for i in range(3):
            spread = jnp.where(target == goal + i, stress[i][y], spread)
        table = jnp.where(place == cells - high * 128, 1.0, 0.0).astype(F32)
        summed = summed + lax.dot_general(
            spread,
            table,
            (((1,), (1,)), ((), ())),
            precision=lax.Precision.HIGHEST,
            preferred_element_type=F32,
        )
    parts[...] = summed.reshape(groups, 8, 128)

    @pl.when(my_grp != 0)
    def _():
        pl.semaphore_wait(all_sem, 1)

    for turn in range(1, groups):
        peer = lax.rem(my_grp + turn, groups)
        pltpu.make_async_remote_copy(
            src_ref=parts.at[peer],
            dst_ref=parts_got.at[turn - 1],
            send_sem=part_send_sem,
            recv_sem=part_recv_sem,
            device_id=(peer, my_aa),
            device_id_type=MESH,
        ).start()

    for c in range(FIRST, SECOND):
        finish_chunk(c)

    pltpu.make_async_copy(parts_got, parts_got, part_recv_sem).wait()
    summed = parts[my_grp]
    for turn in range(1, groups):
        summed = summed + parts_got[turn - 1]
    forcing[:, 0:128] = summed[0:3]
    forcing[:, 128:256] = summed[3:6]

    for c in range(SECOND, last):
        finish_chunk(c)

    @pl.when(is_low)
    def _():
        arrived.wait()
        home.start()
        home.wait_send()

    @pl.when(is_middle)
    def _():
        onward.wait_send()

    pltpu.make_async_copy(parts_got, parts_got, part_send_sem).wait()
    for d in range(2):
        tile(d).wait_send()
        edge(d).wait_send()
        whole = got.at[d, :, pl.ds(SKIP[d], 32 - SKIP[d])]
        pltpu.make_async_copy(whole, whole, send_sem.at[d]).wait()


def pass_on(new, forcing, new_out, forcing_out, sem):
    step = -(-new.shape[0] // PIECES)
    pairs = [(forcing, forcing_out)]
    for i in range(PIECES):
        where = pl.ds(i * step, min(step, new.shape[0] - i * step))
        pairs.append((new.at[where], new_out.at[where]))
    stores = [pltpu.make_async_copy(src, dst, sem.at[i]) for i, (src, dst) in enumerate(pairs)]
    for copy in stores:
        copy.start()
    for copy in stores:
        copy.wait()


def on_device(groups, spectrum, friction, wind_dir, wet, owner, cell):
    comps, rows, width = spectrum.shape
    freqs = comps // DIRS
    chunks = CHUNKS if CHUNKS[-1] == freqs else tuple(range(0, freqs + 1, 2))
    last = len(chunks) - 1
    anywhere = pl.BlockSpec(memory_space=pl.ANY)
    dma = pltpu.SemaphoreType.DMA
    results = (
        jax.ShapeDtypeStruct((freqs, 2 * DIRS, width), F32),
        jax.ShapeDtypeStruct((3, 256), F32),
    )
    vmem = pltpu.VMEM
    inside = pl.BlockSpec(memory_space=pltpu.VMEM)
    new, forcing = pl.pallas_call(
        functools.partial(kernel, chunks),
        out_shape=(vmem((freqs, 2 * DIRS, width), F32), vmem((3, 256), F32)),
        in_specs=[anywhere] * 6,
        out_specs=(inside, inside),
        scratch_shapes=[
            vmem((freqs, 2 * DIRS, width), F32),
            vmem((rows, width), F32),
            vmem((rows, width), F32),
            vmem((8, width), jnp.int32),
            vmem((rows, width), jnp.int32),
            vmem((rows, width), jnp.int32),
            vmem((2, freqs, DIRS, width), F32),
            vmem((chunks[last] - chunks[last - 1], DIRS, width), F32),
            vmem((freqs, 4, 8, width), F32),
            vmem((freqs, 4, 8, width), F32),
            vmem((8, width), F32),
            vmem((2, 8, width), F32),
            vmem((5, 8, 8, width), F32),
            vmem((5, 8, 8, width), F32),
            vmem((2, (freqs + 7) // 8 * 8, width), F32),
            vmem((24, 8, width), F32),
            vmem((2, 16, width), F32),
            vmem((2, 16, width), F32),
            vmem((groups, 8, width), F32),
            vmem((groups - 1, 8, width), F32),
            dma((2,)),
            dma((5,)),
            dma((2,)),
            dma((2, last)),
            dma((2,)),
            dma((2,)),
            dma((2,)),
            dma((2,)),
            dma,
            dma,
            dma,
            dma,
            pltpu.SemaphoreType.REGULAR((2,)),
            pltpu.SemaphoreType.REGULAR,
            pltpu.SemaphoreType.REGULAR,
        ],
        compiler_params=pltpu.CompilerParams(
            collective_id=0, has_side_effects=True, vmem_limit_bytes=LIMIT
        ),
    )(
        spectrum.reshape(freqs, 2 * DIRS, width),
        friction,
        wind_dir,
        wet,
        owner.reshape(rows, width),
        cell,
    )
    new, forcing = pl.pallas_call(
        pass_on,
        out_shape=results,
        in_specs=[inside] * 2,
        out_specs=(anywhere, anywhere),
        scratch_shapes=[dma((PIECES + 1,))],
        compiler_params=pltpu.CompilerParams(vmem_limit_bytes=4 * 1024 * 1024),
    )(new, forcing)
    return new.reshape(comps, rows, width), forcing


def solution(mesh):
    placed = (
        P(None, ("grp", "aa"), None),
        P(("grp", "aa"), None),
        P(("grp", "aa"), None),
        P("grp", None),
        P(("grp", "aa"), None),
        P(("grp", "aa"), None),
    )
    return jax.shard_map(
        functools.partial(on_device, mesh.shape["grp"]),
        mesh=mesh,
        in_specs=placed,
        out_specs=(P(None, ("grp", "aa"), None), P(None, ("grp", "aa"))),
        check_vma=False,
    )
```
